256 devices in a mesh: row: 64 (over z, x, core), col: 4 (over y).
Axes of the slice: x: 4, y: 4, z: 8, core: 2. Of those that a mesh axis runs over, the one named last changes fastest.
Arguments:
- panel: float32 [32768, 16384], P('row', 'col'), may hold values from -180 to 180, as said below
- sketch_matrix: float32 [16384, 512], P('col'), may hold values from -0.046875 to 0.046875
Outputs:
- projected: float32 [512, 16384], P('row', 'col')
- spread: float32 [512, 512], P('row')
The draws below stay inside these ranges and needn't reach their ends.
Inputs may be any that keep to these rules, and one draw needn't show every extreme that they name: `panel`: activation rows with a spread of scales over rows and features.
All inputs are finite; a program needn't handle non-finite values.
Results may differ from the reference program's by a relative error of at most 0.00015.
Values sent between devices are 32-bit elements; how exact they have to be, the bound alone decides.
No kernel may reach another device: no remote copies, remote signals or barrier semaphores. Data moves between devices by JAX's collectives and lax.ppermute only.
A program may use at most 128 MiB of HBM per device.

```python
import math
import jax
import jax.numpy as jnp
from jax import lax

COLS = 16384
RANK = 512
ROWS = 32768


def draw_panel(key, part):
    key = jax.random.fold_in(key, 11)
    key_rows, key_cols, key_noise = jax.random.split(key, 3)
    positions = jnp.arange(ROWS, dtype=jnp.float32)
    rising = jnp.exp(math.log(3.0) * (positions / ROWS - 0.5))
    row_scale = rising * jnp.exp(jax.random.uniform(key_rows, (ROWS,), jnp.float32, math.log(0.5), math.log(5.0)))
    col_scale = jnp.exp(jax.random.uniform(key_cols, (COLS,), jnp.float32, math.log(0.5), math.log(5.0)))
    base_part = jnp.clip(jax.random.normal(key_noise, (ROWS, COLS), jnp.float32), -4.0, 4.0)
    return (base_part * row_scale[:, None] * col_scale[None, :]).astype(jnp.float32)


def block_levels(own_key, dims, cuts, low, largest):
    level, own = 1.0, jax.random.fold_in(own_key, 6)
    for dim, blocks in cuts:
        heights = jnp.exp(jax.random.uniform(jax.random.fold_in(own, dim), (blocks,), jnp.float32, low / len(cuts), largest / len(cuts)))
        level = level * jnp.repeat(heights, dims[dim] // blocks).reshape([-1 if axis == dim else 1 for axis in range(len(dims))])
    return level


def normal_values(key, extent, width, limit, cuts=(), held_as=jnp.bfloat16):
    values = jax.random.normal(key, extent, jnp.float32) * width
    if len(cuts) > 0:
        values = block_levels(key, extent, cuts, -0.22, 0.18) * values
    return jnp.clip(values, min=-limit, max=limit).astype(held_as)


def setup_inputs(seed: int = 0) -> dict:
    key_list = jax.random.split(jax.random.key(seed), 3)
    return {
        "panel": draw_panel(jax.random.fold_in(key_list[2], 71), 0),
        "sketch_matrix": normal_values(key_list[1], (COLS, RANK), COLS ** -0.5, 0.046875, ((0, 4),), jnp.float32),
    }


def reference(panel, sketch_matrix):
    highest = lax.Precision.HIGHEST
    sketch = jnp.dot(panel.astype(jnp.float32), sketch_matrix.astype(jnp.float32), preferred_element_type=jnp.float32, precision=highest)
    gram_sum = jnp.dot(sketch.T.astype(jnp.float32), sketch.astype(jnp.float32), preferred_element_type=jnp.float32, precision=highest)
    lower_factor = jnp.linalg.cholesky(gram_sum)
    basis_t = jax.scipy.linalg.solve_triangular(lower_factor, sketch.T, lower=True)
    norm_scale = 1.0 / math.sqrt(ROWS)
    projected = jnp.dot(basis_t.astype(jnp.float32), panel.astype(jnp.float32), preferred_element_type=jnp.float32, precision=highest) * norm_scale
    spread = lower_factor.T * norm_scale
    return (projected, spread)
```

```python
import math

import jax
import jax.numpy as jnp
from jax import lax
from jax.sharding import PartitionSpec as P

HIGH = lax.Precision.HIGH
ZS, XS, CS = 8, 4, 2


def mm(left, right, dims):
    return lax.dot_general(
        left, right, (dims, ((), ())), precision=HIGH, preferred_element_type=jnp.float32
    )


def row_index(z, x, c):
    return ((z % ZS) * XS + x % XS) * CS + c


def row_pairs(move):
    return [
        (row_index(z, x, c), row_index(*move(z, x, c)))
        for z in range(ZS)
        for x in range(XS)
        for c in range(CS)
    ]


def send_z(array, step):
    return lax.ppermute(array, "row", row_pairs(lambda z, x, c: (z + step, x, c)))


def send_x(array, step):
    return lax.ppermute(array, "row", row_pairs(lambda z, x, c: (z, x + step, c)))


def swap_z(array, bit):
    return lax.ppermute(array, "row", row_pairs(lambda z, x, c: (z ^ bit, x, c)))


def swap_core(array):
    return lax.ppermute(array, "row", row_pairs(lambda z, x, c: (z, x, 1 - c)))


def send_y(array, step):
    return lax.ppermute(array, "col", [(i, (i + step) % 4) for i in range(4)])


def ring_reduce_scatter(chunk, size, send):
    far = size // 2
    block = chunk(far)
    half = block.shape[0] // 2
    ahead, behind = send(block[:half], 1), send(block[half:], -1)
    for k in range(far - 1, 0, -1):
        first, second = chunk(k), chunk(-k)
        if k == far - 1:
            first = jnp.concatenate([first[:half] + ahead, first[half:]], 0)
            second = jnp.concatenate([second[:half], second[half:] + behind], 0)
        else:
            first, second = first + ahead, second + behind
        ahead, behind = send(first, 1), send(second, -1)
    return chunk(0) + ahead + behind


def ring_all_gather(own, size, send):
    far = size // 2
    half = own.shape[0] // 2
    blocks = {0: own}
    from_behind = from_ahead = own
    for k in range(1, far):
        from_behind, from_ahead = send(from_behind, 1), send(from_ahead, -1)
        blocks[-k], blocks[k] = from_behind, from_ahead
    blocks[far] = jnp.concatenate(
        [send(from_behind[:half], 1), send(from_ahead[half:], -1)], 0
    )
    return blocks


def place(blocks, size, position):
    own = blocks[0]
    out = jnp.zeros((size,) + own.shape, own.dtype)
    for k, block in blocks.items():
        out = lax.dynamic_update_index_in_dim(out, block, (position + k) % size, 0)
    return out


def shards(panel, sketch_matrix):
    rank = sketch_matrix.shape[1]
    local_rows, local_cols = panel.shape
    total_rows = local_rows * lax.axis_size("row")
    norm_scale = 1.0 / math.sqrt(total_rows)
    row = lax.axis_index("row")
    z, x, c = row // (XS * CS), (row // CS) % XS, row % CS
    y = lax.axis_index("col")

    with jax.named_scope("sketch"):
        partial = mm(panel, sketch_matrix, ((1,), (0,)))
        part = local_rows // 4

        def sketch_chunk(k):
            return lax.dynamic_slice_in_dim(partial, ((y + k) % 4) * part, part, 0)

        own_sketch = ring_reduce_scatter(sketch_chunk, 4, send_y)
        sketch = place(ring_all_gather(own_sketch, 4, send_y), 4, y)
        sketch = sketch.reshape(local_rows, rank)

    with jax.named_scope("gram"):
        share = rank // 4
        own_cols = lax.dynamic_slice_in_dim(sketch, y * share, share, 1)
        gram = mm(own_cols, sketch, ((0,), (0,)))
        half = share // CS
        gram = lax.dynamic_slice_in_dim(gram, c * half, half, 0) + swap_core(
            lax.dynamic_slice_in_dim(gram, (1 - c) * half, half, 0)
        )
        quarter = half // XS
        gram = ring_reduce_scatter(
            lambda k: lax.dynamic_slice_in_dim(gram, ((x + k) % XS) * quarter, quarter, 0),
            XS,
            send_x,
        )
        for bit in (1, 2, 4):
            gram = gram + swap_z(gram, bit)
        gram = place(ring_all_gather(gram, 4, send_y), 4, y)
        gram = place(ring_all_gather(gram, XS, send_x), XS, x)
        gram = place({0: gram, 1: swap_core(gram)}, CS, c)
        gram = gram.transpose(2, 0, 1, 3, 4).reshape(rank, rank)

    with jax.named_scope("factor"):
        lower = jnp.linalg.cholesky(gram)
        inverse = jax.scipy.linalg.solve_triangular(
            lower, jnp.eye(rank, dtype=jnp.float32), lower=True
        )

    with jax.named_scope("project"):
        half_cols = local_cols // CS
        other = lax.dynamic_slice_in_dim(panel, (1 - c) * half_cols, half_cols, 1)
        mine = lax.dynamic_slice_in_dim(panel, c * half_cols, half_cols, 1)
        arrived = swap_core(mm(other, sketch, ((0,), (0,))))
        total = mm(mine, sketch, ((0,), (0,))) + arrived
        x_cols = half_cols // XS
        total = ring_reduce_scatter(
            lambda k: lax.dynamic_slice_in_dim(total, ((x + k) % XS) * x_cols, x_cols, 0),
            XS,
            send_x,
        )
        z_cols = x_cols // ZS
        total = ring_reduce_scatter(
            lambda k: lax.dynamic_slice_in_dim(total, ((z + k) % ZS) * z_cols, z_cols, 0),
            ZS,
            send_z,
        )
        total = place(ring_all_gather(total, ZS, send_z), ZS, z).reshape(x_cols, rank)

    with jax.named_scope("apply"):
        z_rows = rank // ZS
        z_inverse = lax.dynamic_slice_in_dim(inverse, z * z_rows, z_rows, 0)
        result = mm(z_inverse, total, ((1,), (1,))) * norm_scale
        share = z_rows // (XS * CS)
        result = result.reshape(XS, CS, share, x_cols)
        arrived = swap_core(lax.dynamic_index_in_dim(result, 1 - c, 1, keepdims=False))
        kept = lax.dynamic_index_in_dim(result, c, 1, keepdims=False)
        both = place({0: kept, 1: arrived}, CS, c)
        blocks = {0: lax.dynamic_index_in_dim(both, x, 1, keepdims=False)}
        for k in (1, 2, 3):
            blocks[-k] = send_x(
                lax.dynamic_index_in_dim(both, (x + k) % XS, 1, keepdims=False), k
            )
        blocks = place(blocks, XS, x)
        projected = blocks.transpose(2, 1, 0, 3).reshape(share, local_cols)
        row_share = rank // (ZS * XS * CS)
        spread = (
            lax.dynamic_slice_in_dim(lower, row * row_share, row_share, 1).T * norm_scale
        )
    return (projected, spread)


def solution(mesh):
    return jax.shard_map(
        shards,
        mesh=mesh,
        in_specs=(P("row", "col"), P("col", None)),
        out_specs=(P("row", "col"), P("row", None)),
        check_vma=False,
    )
```

```python
import functools
import math

import jax
import jax.numpy as jnp
from jax import lax
from jax.experimental import pallas as pl
from jax.experimental.pallas import tpu as pltpu
from jax.sharding import PartitionSpec as P

ZS, XS, CS, YS = 8, 4, 2, 4
BLOCK = 128
PIVOTS = 32
WIDTH = 512
F32, BF16 = jnp.float32, jnp.bfloat16


def row_index(z, x, c):
    return ((z % ZS) * XS + x % XS) * CS + c


def row_pairs(move):
    return [
        (row_index(z, x, c), row_index(*move(z, x, c)))
        for z in range(ZS)
        for x in range(XS)
        for c in range(CS)
    ]


Z_GROUPS = [[row_index(z, x, c) for z in range(ZS)] for x in range(XS) for c in range(CS)]
ZX_GROUPS = [[row_index(z, x, c) for z in range(ZS) for x in range(XS)] for c in range(CS)]


def send_y(array, step):
    return lax.ppermute(array, "col", [(i, (i + step) % YS) for i in range(YS)])


def swap_core(array):
    return lax.ppermute(array, "row", row_pairs(lambda z, x, c: (z, x, 1 - c)))


def exchange(array, groups):
    return lax.all_to_all(array, "row", 0, 0, axis_index_groups=groups)


def repeat(array, times):
    return jnp.broadcast_to(array[None], (times,) + array.shape)


def together(*arrays):
    return lax.optimization_barrier(arrays)


def ring_sum_y(ahead, behind, next_head, before_tail, own):
    half = own.shape[0] // 2
    from_before, from_after = together(send_y(ahead, 1), send_y(behind, -1))
    head, tail = together(next_head + from_before[:half], before_tail + from_after[half:])
    head, tail = together(send_y(head, 1), send_y(tail, -1))
    return own + jnp.concatenate([from_after[:half] + head, from_before[half:] + tail], 0)


def ring_gather_y(own):
    half = own.shape[0] // 2
    before, after = together(send_y(own, 1), send_y(own, -1))
    return own, before, after, send_y(before[:half], 1), send_y(after[half:], -1)


def place(blocks, size, position):
    own = blocks[0]
    out = jnp.zeros((size,) + own.shape, own.dtype)
    for k, block in blocks.items():
        out = lax.dynamic_update_index_in_dim(out, block, (position + k) % size, 0)
    return out


def split(array):
    high = array.astype(BF16)
    return high, (array - high.astype(F32)).astype(BF16)


def dot(left, right):
    return jnp.dot(left, right, preferred_element_type=F32)


def dot_parts(left, right):
    return dot(left[0], right[0]) + dot(left[0], right[1]) + dot(left[1], right[0])


def params(size):
    return pltpu.CompilerParams(vmem_limit_bytes=size * 2**20)


def cost(flops, size):
    return pl.CostEstimate(flops=flops, bytes_accessed=size, transcendentals=0)


IN_VMEM = pl.BlockSpec(memory_space=pltpu.VMEM)
IN_PLACE = pl.BlockSpec(memory_space=pl.ANY)
IN_SMEM = pl.BlockSpec(memory_space=pltpu.SMEM)


def sketch_kernel(
    y_ref, panel_ref, matrix_ref, ahead_ref, behind_ref, next_ref, before_ref, own_ref,
    panels, matrices, total, panel_sems, matrix_sems,
):
    steps, _, width = panels.shape

    def copies(k):
        at = pl.ds(pl.multiple_of(k * width, width), width)
        return (
            pltpu.make_async_copy(panel_ref.at[:, at], panels.at[k], panel_sems.at[k]),
            pltpu.make_async_copy(matrix_ref.at[at], matrices.at[k], matrix_sems.at[k]),
        )

    for k in range(steps):
        for copy in copies(k):
            copy.start()
    total[...] = jnp.zeros_like(total)

    def step(k, carry):
        for copy in copies(k):
            copy.wait()
        total[...] += dot_parts(split(panels[k]), split(matrices[k]))
        return carry

    lax.fori_loop(0, steps, step, 0)
    block = own_ref.shape[0]
    half = block // 2

    def rows(step, start, size):
        at = lax.rem(y_ref[0] + step, YS) * block + start
        return total[pl.ds(pl.multiple_of(at, half), size), :]

    ahead_ref[:half] = rows(2, 0, half)
    ahead_ref[half:] = rows(1, half, half)
    behind_ref[:half] = rows(3, 0, half)
    behind_ref[half:] = rows(2, half, half)
    next_ref[...] = rows(1, 0, half)
    before_ref[...] = rows(3, half, half)
    own_ref[...] = rows(0, 0, block)


def sketch_product(y, panel, matrix):
    rows, depth = panel.shape
    rank = matrix.shape[1]
    steps = depth // WIDTH
    block = rows // YS
    whole = jax.ShapeDtypeStruct((block, rank), F32)
    half = jax.ShapeDtypeStruct((block // 2, rank), F32)
    return pl.pallas_call(
        sketch_kernel,
        in_specs=[IN_SMEM, IN_PLACE, IN_PLACE],
        out_specs=(IN_VMEM,) * 5,
        out_shape=(whole, whole, half, half, whole),
        scratch_shapes=[
            pltpu.VMEM((steps, rows, WIDTH), F32),
            pltpu.VMEM((steps, WIDTH, rank), F32),
            pltpu.VMEM((rows, rank), F32),
            pltpu.SemaphoreType.DMA((steps,)),
            pltpu.SemaphoreType.DMA((steps,)),
        ],
        compiler_params=params(54),
        cost_estimate=cost(6 * rows * rank * depth, 4 * depth * (rows + rank)),
        name="sketch_product",
    )(y, panel, matrix)


def place_kernel(y_ref, own, before, after, head, tail, out_ref):
    y = y_ref[0]
    at = lambda step: lax.rem(y + step, YS)
    half = out_ref.shape[1] // 2
    out_ref[at(0)] = own[...]
    out_ref[at(3)] = before[...]
    out_ref[at(1)] = after[...]
    out_ref[at(2), :half] = head[...]
    out_ref[at(2), half:] = tail[...]


def place_blocks(y, blocks):
    rows, rank = blocks[0].shape
    return pl.pallas_call(
        place_kernel,
        in_specs=[IN_SMEM] + [IN_VMEM] * 5,
        out_specs=IN_VMEM,
        out_shape=jax.ShapeDtypeStruct((YS, rows, rank), F32),
        compiler_params=params(16),
        cost_estimate=cost(0, 8 * YS * rows * rank),
        name="place_blocks",
    )(y, *blocks).reshape(YS * rows, rank)


def gram_kernel(
    y_ref, core_ref, own_ref, other_ref, gram_ref, own_high, own_low, other_high, other_low,
    parts, turned, sems,
):
    outs = (own_high, own_low, other_high, other_low)
    leave = lambda k: pltpu.make_async_copy(parts.at[k], outs[k], sems.at[k])
    share = gram_ref.shape[0]
    total = None
    for k, sketch_ref in enumerate((own_ref, other_ref)):
        sketch = sketch_ref[...]
        high, low = split(sketch)
        parts[2 * k] = high
        parts[2 * k + 1] = low
        leave(2 * k).start()
        leave(2 * k + 1).start()
        block = CS * share
        columns = pl.ds(pl.multiple_of(y_ref[0] * block, block), block)
        turned[...] = sketch_ref[:, columns].T
        rows = turned[pl.ds(pl.multiple_of(core_ref[0] * share, share), share), :]
        term = dot_parts(split(rows), (high, low))
        total = term if total is None else total + term
    gram_ref[...] = total
    for k in range(4):
        leave(k).wait()


def gram_product(y, core, own, other):
    rows, rank = own.shape
    share = rank // (YS * CS)
    part = jax.ShapeDtypeStruct((rows, rank), BF16)
    return pl.pallas_call(
        gram_kernel,
        in_specs=[IN_SMEM, IN_SMEM, IN_VMEM, IN_VMEM],
        out_specs=(IN_VMEM,) + (IN_PLACE,) * 4,
        out_shape=(jax.ShapeDtypeStruct((share, rank), F32),) + (part,) * 4,
        scratch_shapes=[
            pltpu.VMEM((4, rows, rank), BF16),
            pltpu.VMEM((CS * share, rows), F32),
            pltpu.SemaphoreType.DMA((4,)),
        ],
        compiler_params=params(24),
        cost_estimate=cost(12 * rows * rank * share, 16 * rows * rank),
        name="gram_product",
    )(y, core, own, other)


def project_kernel(
    core_ref, own_high, own_low, other_high, other_low, panel_ref, arrived_ref, out_ref,
    sketches, panels, arrived, outs, sketch_sems, panel_sems, arrived_sems, out_sems,
):
    steps, _, width = panels.shape
    base = core_ref[0] * (steps * width)

    def arrive(k):
        at = pl.ds(pl.multiple_of(base + k * width, width), width)
        return (
            pltpu.make_async_copy(panel_ref.at[:, at], panels.at[k], panel_sems.at[k]),
            pltpu.make_async_copy(arrived_ref.at[:, at], arrived.at[k], arrived_sems.at[k]),
        )

    def leave(k):
        at = pl.ds(pl.multiple_of(k * width, width), width)
        return pltpu.make_async_copy(outs.at[k], out_ref.at[at], out_sems.at[k])

    loads = [
        pltpu.make_async_copy(part, sketches.at[k], sketch_sems.at[k])
        for k, part in enumerate((own_high, own_low, other_high, other_low))
    ]
    for copy in loads:
        copy.start()
    for k in range(steps):
        for copy in arrive(k):
            copy.start()
    for copy in loads:
        copy.wait()

    def step(k, carry):
        for copy in arrive(k):
            copy.wait()
        own = dot_parts(split(panels[k].T), (sketches[0], sketches[1]))
        outs[k] = own + dot_parts(split(arrived[k].T), (sketches[2], sketches[3]))
        leave(k).start()
        return carry

    lax.fori_loop(0, steps, step, 0)
    for k in range(steps):
        leave(k).wait()


def project_product(core, sketches, panel, arrived):
    rows, rank = sketches[0].shape
    cols = panel.shape[1] // CS
    steps = cols // WIDTH
    return pl.pallas_call(
        project_kernel,
        in_specs=[IN_SMEM] + [IN_PLACE] * 6,
        out_specs=IN_PLACE,
        out_shape=jax.ShapeDtypeStruct((cols, rank), F32),
        scratch_shapes=[
            pltpu.VMEM((4, rows, rank), BF16),
            pltpu.VMEM((steps, rows, WIDTH), F32),
            pltpu.VMEM((steps, rows, WIDTH), F32),
            pltpu.VMEM((steps, WIDTH, rank), F32),
            pltpu.SemaphoreType.DMA((4,)),
            pltpu.SemaphoreType.DMA((steps,)),
            pltpu.SemaphoreType.DMA((steps,)),
            pltpu.SemaphoreType.DMA((steps,)),
        ],
        compiler_params=params(57),
        cost_estimate=cost(12 * rank * rows * cols, 12 * cols * (rows + rank)),
        name="project_product",
    )(core, *sketches, panel, arrived)


def exact_dot(left, right, dims):
    return lax.dot_general(
        left, right, (dims, ((), ())), precision=lax.Precision.HIGHEST, preferred_element_type=F32
    )


def eliminate(rows, base):
    tiles = len(rows)
    count = 8 * tiles
    lanes = BLOCK
    sub = lax.broadcasted_iota(jnp.int32, (8, lanes), 0)
    spread = lambda a, u: jnp.broadcast_to(a[u : u + 1, :], (8, lanes))
    columns = [
        [jnp.broadcast_to(row[:, base + t : base + t + 1], (8, lanes)) for row in rows]
        for t in range(count)
    ]
    parts = rows[0].shape[1] // lanes
    rows = [[row[:, lanes * q : lanes * (q + 1)] for q in range(parts)] for row in rows]
    scales = []
    for s in range(count):
        first, u = divmod(s, 8)
        pivot = spread(columns[s][first], u)
        scales.append(lax.rsqrt(pivot))
        inverse = 1.0 / pivot
        factor = {v: columns[s][v] * inverse for v in range(first, tiles)}
        factor[first] = jnp.where(sub > u, factor[first], 0.0)
        for t in range(s + 1, count):
            pivot_row = spread(columns[t][first], u)
            for v in range(first, tiles):
                columns[t][v] = columns[t][v] - factor[v] * pivot_row
        for q in range(parts):
            pivot_row = spread(rows[first][q], u)
            for v in range(first, tiles):
                rows[v][q] = rows[v][q] - factor[v] * pivot_row
    out = []
    for v in range(tiles):
        scale = scales[8 * v]
        for u in range(1, 8):
            scale = jnp.where(sub == u, scales[8 * v + u], scale)
        out.append([part * scale for part in rows[v]])
    return out


def factor_kernel(d, *refs):
    gram_ref, upper, inverse = refs[0], refs[1 : 1 + d], refs[1 + d : 1 + 2 * d]
    upper_ref, inverse_ref, work = refs[1 + 2 * d :]
    rank = gram_ref.shape[1]
    low = BLOCK * d
    here = slice(low, low + BLOCK)
    right = gram_ref[:, low:]
    left = None
    for k in range(d):
        column = upper[k][:, here]
        right = right - exact_dot(column, upper[k][:, low:], ((0,), (0,)))
        term = exact_dot(column, inverse[k][:, :low], ((0,), (0,)))
        left = -term if left is None else left - term
    row_ids = lax.broadcasted_iota(jnp.int32, (BLOCK, BLOCK), 0)
    column_ids = lax.broadcasted_iota(jnp.int32, (BLOCK, BLOCK), 1)
    work[:, :BLOCK] = right[:, :BLOCK]
    work[:, BLOCK:] = (row_ids == column_ids).astype(F32)
    for p in range(0, BLOCK, PIVOTS):
        rows = work[p : p + PIVOTS, :]
        if p:
            rows = rows - exact_dot(work[:p, p : p + PIVOTS], work[:p, :], ((0,), (0,)))
        tiles = [rows[v : v + 8] for v in range(0, PIVOTS, 8)]
        for v, parts in enumerate(eliminate(tiles, p)):
            for q, part in enumerate(parts):
                work[p + 8 * v : p + 8 * v + 8, BLOCK * q : BLOCK * (q + 1)] = part
    block_inverse = work[:, BLOCK:]
    upper_ref[...] = jnp.zeros_like(upper_ref)
    inverse_ref[...] = jnp.zeros_like(inverse_ref)
    upper_ref[:, here] = jnp.where(row_ids <= column_ids, work[:, :BLOCK], 0.0)
    inverse_ref[:, here] = block_inverse
    if low + BLOCK < rank:
        upper_ref[:, low + BLOCK :] = exact_dot(block_inverse, right[:, BLOCK:], ((1,), (0,)))
    if d:
        inverse_ref[:, :low] = exact_dot(block_inverse, left, ((1,), (0,)))


def factor_step(d, gram, upper, inverse):
    rank = gram.shape[1]
    out = jax.ShapeDtypeStruct((BLOCK, rank), F32)
    first = pl.BlockSpec((BLOCK, rank), lambda i: (0, 0))
    return pl.pallas_call(
        functools.partial(factor_kernel, d),
        grid=(1,),
        in_specs=[pl.BlockSpec((BLOCK, rank), lambda i: (d, 0))] + [first] * (2 * d),
        out_specs=(first, first),
        out_shape=(out, out),
        scratch_shapes=[pltpu.VMEM((BLOCK, 2 * BLOCK), F32)],
        compiler_params=params(24),
        cost_estimate=cost(5_000_000_000, 4 * BLOCK * rank * (2 * d + 3)),
        name="factor_step",
    )(gram, *upper, *inverse)


def factorize(gram):
    upper, inverse = [], []
    for d in range(gram.shape[0] // BLOCK):
        up, inv = factor_step(d, gram, upper, inverse)
        upper.append(up)
        inverse.append(inv)
    return jnp.concatenate(upper, 0), jnp.concatenate(inverse, 0)


def shards(panel, sketch_matrix):
    rank = sketch_matrix.shape[1]
    local_rows, local_cols = panel.shape
    total_rows = local_rows * lax.axis_size("row")
    norm_scale = 1.0 / math.sqrt(total_rows)
    row = lax.axis_index("row")
    c = row % CS
    core, y = c.reshape(1), lax.axis_index("col").reshape(1)
    row_share = rank // (ZS * XS * CS)

    with jax.named_scope("sketch"):
        arrived = swap_core(panel)
        pieces = sketch_product(y, panel, sketch_matrix)
        own = place_blocks(y, ring_gather_y(ring_sum_y(*pieces)))
        other = swap_core(own)

    with jax.named_scope("gram"):
        gram, *sketches = gram_product(y, core, own, other)
        gram, *sketches = together(gram, *sketches)
        gram = exchange(gram.reshape(ZS * XS, -1, rank), ZX_GROUPS)

    with jax.named_scope("project"):
        total = project_product(core, sketches, panel, arrived)
        total = lax.psum_scatter(
            total, "row", scatter_dimension=0, axis_index_groups=Z_GROUPS, tiled=True
        )

    with jax.named_scope("gram"):
        gram = exchange(repeat(gram.sum(0), ZS * XS), ZX_GROUPS).reshape(-1, rank)
        gram = place_blocks(y, ring_gather_y(gram)).reshape(YS, -1, rank)
        gram = place({0: gram, 1: swap_core(gram)}, CS, c)
        gram = gram.transpose(1, 0, 2, 3).reshape(rank, rank)

    with jax.named_scope("factor"):
        upper, inverse = factorize(gram)

    with jax.named_scope("apply"):
        result = lax.dot_general(
            inverse,
            total,
            (((1,), (1,)), ((), ())),
            precision=lax.Precision.HIGH,
            preferred_element_type=F32,
        )
        width = result.shape[1]
        result = exchange(result.reshape(-1, row_share, width), None)
        result = result.reshape(ZS, XS, CS, row_share, width).sum(1) * norm_scale
        projected = result.transpose(2, 1, 0, 3).reshape(row_share, local_cols)
        spread = lax.dynamic_slice_in_dim(upper, row * row_share, row_share, 0) * norm_scale
    return (projected, spread)


def solution(mesh):
    return jax.shard_map(
        shards,
        mesh=mesh,
        in_specs=(P("row", "col"), P("col", None)),
        out_specs=(P("row", "col"), P("row", None)),
        check_vma=False,
    )
```

```python
import functools
import math

import jax
import jax.numpy as jnp
from jax import lax
from jax.experimental import pallas as pl
from jax.experimental.pallas import tpu as pltpu
from jax.sharding import PartitionSpec as P

ZS, XS, CS, YS = 8, 4, 2, 4
BLOCK = 128
PIVOTS = 32
WIDTH = 512
F32, BF16 = jnp.float32, jnp.bfloat16


def row_index(z, x, c):
    return ((z % ZS) * XS + x % XS) * CS + c


def row_pairs(move):
    return [
        (row_index(z, x, c), row_index(*move(z, x, c)))
        for z in range(ZS)
        for x in range(XS)
        for c in range(CS)
    ]


Z_GROUPS = [[row_index(z, x, c) for z in range(ZS)] for x in range(XS) for c in range(CS)]
ZX_GROUPS = [[row_index(z, x, c) for z in range(ZS) for x in range(XS)] for c in range(CS)]


def send_y(array, step):
    return lax.ppermute(array, "col", [(i, (i + step) % YS) for i in range(YS)])


def swap_core(array):
    return lax.ppermute(array, "row", row_pairs(lambda z, x, c: (z, x, 1 - c)))


def exchange(array, groups):
    return lax.all_to_all(array, "row", 0, 0, axis_index_groups=groups)


def repeat(array, times):
    return jnp.broadcast_to(array[None], (times,) + array.shape)


def together(*arrays):
    return lax.optimization_barrier(arrays)


def ring_sum_y(ahead, behind, next_head, before_tail, own):
    half = own.shape[0] // 2
    from_before, from_after = together(send_y(ahead, 1), send_y(behind, -1))
    head, tail = together(next_head + from_before[:half], before_tail + from_after[half:])
    head, tail = together(send_y(head, 1), send_y(tail, -1))
    return own + jnp.concatenate([from_after[:half] + head, from_before[half:] + tail], 0)


def ring_gather_y(own):
    half = own.shape[0] // 2
    before, after = together(send_y(own, 1), send_y(own, -1))
    return own, before, after, send_y(before[:half], 1), send_y(after[half:], -1)


def place(blocks, size, position):
    own = blocks[0]
    out = jnp.zeros((size,) + own.shape, own.dtype)
    for k, block in blocks.items():
        out = lax.dynamic_update_index_in_dim(out, block, (position + k) % size, 0)
    return out


def split(array):
    high = array.astype(BF16)
    return high, (array - high.astype(F32)).astype(BF16)


def dot(left, right):
    return jnp.dot(left, right, preferred_element_type=F32)


def dot_parts(left, right):
    return dot(left[0], right[0]) + dot(left[0], right[1]) + dot(left[1], right[0])


def params(size):
    return pltpu.CompilerParams(vmem_limit_bytes=size * 2**20)


def cost(flops, size):
    return pl.CostEstimate(flops=flops, bytes_accessed=size, transcendentals=0)


IN_VMEM = pl.BlockSpec(memory_space=pltpu.VMEM)
IN_PLACE = pl.BlockSpec(memory_space=pl.ANY)
IN_SMEM = pl.BlockSpec(memory_space=pltpu.SMEM)


def sketch_kernel(pieces, y_ref, panel_ref, matrix_ref, *refs):
    out_refs, (panels, matrices, total, panel_sems, matrix_sems) = refs[:-5], refs[-5:]
    steps, _, width = panels.shape
    block = panel_ref.shape[0] // YS

    def copies(k):
        at = pl.ds(pl.multiple_of(k * width, width), width)
        out = [pltpu.make_async_copy(matrix_ref.at[at], matrices.at[k], matrix_sems.at[k])]
        offset = 0
        for i, (step, start, size) in enumerate(pieces):
            row = lax.rem(y_ref[0] + step, YS) * block + start
            out.append(
                pltpu.make_async_copy(
                    panel_ref.at[pl.ds(pl.multiple_of(row, block // 2), size), at],
                    panels.at[k, pl.ds(offset, size)],
                    panel_sems.at[k, i],
                )
            )
            offset += size
        return out

    for k in range(steps):
        for copy in copies(k):
            copy.start()
    total[...] = jnp.zeros_like(total)

    def step(k, carry):
        for copy in copies(k):
            copy.wait()
        total[...] += dot_parts(split(panels[k]), split(matrices[k]))
        return carry

    lax.fori_loop(0, steps, step, 0)
    offset = 0
    for out_ref in out_refs:
        size = out_ref.shape[0]
        out_ref[...] = total[offset : offset + size]
        offset += size


def sketch_product(y, panel, matrix, pieces, sizes):
    depth = panel.shape[1]
    rows = sum(sizes)
    rank = matrix.shape[1]
    steps = depth // WIDTH
    return pl.pallas_call(
        functools.partial(sketch_kernel, pieces),
        in_specs=[IN_SMEM, IN_PLACE, IN_PLACE],
        out_specs=(IN_VMEM,) * len(sizes),
        out_shape=tuple(jax.ShapeDtypeStruct((size, rank), F32) for size in sizes),
        scratch_shapes=[
            pltpu.VMEM((steps, rows, WIDTH), F32),
            pltpu.VMEM((steps, WIDTH, rank), F32),
            pltpu.VMEM((rows, rank), F32),
            pltpu.SemaphoreType.DMA((steps, len(pieces))),
            pltpu.SemaphoreType.DMA((steps,)),
        ],
        compiler_params=params(54),
        cost_estimate=cost(6 * rows * rank * depth, 4 * depth * (rows + rank)),
        name="sketch_product",
    )(y, panel, matrix)


def place_kernel(y_ref, own, before, after, head, tail, placed):
    y = y_ref[0]
    at = lambda step: lax.rem(y + step, YS)
    half = placed.shape[1] // 2
    placed[at(0)] = own[...]
    placed[at(3)] = before[...]
    placed[at(1)] = after[...]
    placed[at(2), :half] = head[...]
    placed[at(2), half:] = tail[...]


def place_blocks(y, blocks):
    rows, rank = blocks[0].shape
    return pl.pallas_call(
        place_kernel,
        in_specs=[IN_SMEM] + [IN_VMEM] * 5,
        out_specs=IN_VMEM,
        out_shape=jax.ShapeDtypeStruct((YS, rows, rank), F32),
        compiler_params=params(24),
        cost_estimate=cost(0, 8 * YS * rows * rank),
        name="place_blocks",
    )(y, *blocks).reshape(YS * rows, rank)


def chip_kernel(
    y_ref, core_ref, own_ref, other_ref, panel_ref, arrived_ref, gram_ref, out_ref,
    parts, turned, gram, panels, arrived, outs, panel_sems, arrived_sems, out_sems,
):
    steps, _, width = panels.shape
    base = core_ref[0] * (steps * width)

    def arrive(k):
        at = pl.ds(pl.multiple_of(base + k * width, width), width)
        return (
            pltpu.make_async_copy(panel_ref.at[:, at], panels.at[k], panel_sems.at[k]),
            pltpu.make_async_copy(arrived_ref.at[:, at], arrived.at[k], arrived_sems.at[k]),
        )

    def leave(k):
        at = pl.ds(pl.multiple_of(k * width, width), width)
        return pltpu.make_async_copy(outs.at[k], out_ref.at[at], out_sems.at[k])

    for k in range(steps):
        for copy in arrive(k):
            copy.start()
    share = gram.shape[0]
    block = CS * share
    columns = pl.ds(pl.multiple_of(y_ref[0] * block, block), block)
    for k, sketch_ref in enumerate((own_ref, other_ref)):
        high, low = split(sketch_ref[...])
        parts[2 * k] = high
        parts[2 * k + 1] = low
        turned[...] = sketch_ref[:, columns].T
        rows = turned[pl.ds(pl.multiple_of(core_ref[0] * share, share), share), :]
        term = dot_parts(split(rows), (high, low))
        if k == 0:
            gram[...] = term
        else:
            gram[...] += term
    size = gram_ref.shape[1]
    for k in range(gram_ref.shape[0]):
        gram_ref[k] = gram[size * k : size * (k + 1), :]

    def step(k, carry):
        for copy in arrive(k):
            copy.wait()
        own = dot_parts(split(panels[k].T), (parts[0], parts[1]))
        outs[k] = own + dot_parts(split(arrived[k].T), (parts[2], parts[3]))
        leave(k).start()
        return carry

    lax.fori_loop(0, steps, step, 0)
    for k in range(steps):
        leave(k).wait()


def chip_products(y, core, own, other, panel, arrived):
    rows, rank = own.shape
    share = rank // (YS * CS)
    cols = panel.shape[1] // CS
    steps = cols // WIDTH
    return pl.pallas_call(
        chip_kernel,
        in_specs=[IN_SMEM] * 2 + [IN_VMEM] * 2 + [IN_PLACE] * 2,
        out_specs=(IN_VMEM, IN_PLACE),
        out_shape=(
            jax.ShapeDtypeStruct((ZS * XS, share // (ZS * XS), rank), F32),
            jax.ShapeDtypeStruct((cols, rank), F32),
        ),
        scratch_shapes=[
            pltpu.VMEM((2 * CS, rows, rank), BF16),
            pltpu.VMEM((CS * share, rows), F32),
            pltpu.VMEM((share, rank), F32),
            pltpu.VMEM((steps, rows, WIDTH), F32),
            pltpu.VMEM((steps, rows, WIDTH), F32),
            pltpu.VMEM((steps, WIDTH, rank), F32),
            pltpu.SemaphoreType.DMA((steps,)),
            pltpu.SemaphoreType.DMA((steps,)),
            pltpu.SemaphoreType.DMA((steps,)),
        ],
        compiler_params=params(57),
        cost_estimate=cost(12 * rank * rows * cols, 12 * cols * (rows + rank)),
        name="chip_products",
    )(y, core, own, other, panel, arrived)


def exact_dot(left, right, dims):
    return lax.dot_general(
        left, right, (dims, ((), ())), precision=lax.Precision.HIGHEST, preferred_element_type=F32
    )


def eliminate(rows, base):
    tiles = len(rows)
    count = 8 * tiles
    lanes = BLOCK
    sub = lax.broadcasted_iota(jnp.int32, (8, lanes), 0)
    spread = lambda a, u: jnp.broadcast_to(a[u : u + 1, :], (8, lanes))
    columns = [
        [jnp.broadcast_to(row[:, base + t : base + t + 1], (8, lanes)) for row in rows]
        for t in range(count)
    ]
    parts = rows[0].shape[1] // lanes
    rows = [[row[:, lanes * q : lanes * (q + 1)] for q in range(parts)] for row in rows]
    scales = []
    for s in range(count):
        first, u = divmod(s, 8)
        if s == 0:
            pivot = spread(columns[0][0], 0)
        scales.append(lax.rsqrt(pivot))
        inverse = 1.0 / pivot
        if s + 1 < count:
            after, at = divmod(s + 1, 8)
            beside = spread(columns[s][after], at)
            pivot = spread(columns[s + 1][after], at) - (beside * inverse) * beside
        factor = {v: columns[s][v] * inverse for v in range(first, tiles)}
        factor[first] = jnp.where(sub > u, factor[first], 0.0)
        for t in range(s + 1, count):
            pivot_row = spread(columns[t][first], u)
            for v in range(first, tiles):
                columns[t][v] = columns[t][v] - factor[v] * pivot_row
        for q in range(parts):
            pivot_row = spread(rows[first][q], u)
            for v in range(first, tiles):
                rows[v][q] = rows[v][q] - factor[v] * pivot_row
    out = []
    for v in range(tiles):
        scale = scales[8 * v]
        for u in range(1, 8):
            scale = jnp.where(sub == u, scales[8 * v + u], scale)
        out.append([part * scale for part in rows[v]])
    return out


def factor_kernel(d, *refs):
    gram_ref, upper, inverse = refs[0], refs[1 : 1 + d], refs[1 + d : 1 + 2 * d]
    upper_ref, inverse_ref, work = refs[1 + 2 * d :]
    rank = gram_ref.shape[1]
    low = BLOCK * d
    here = slice(low, low + BLOCK)
    right = gram_ref[here, low:]
    left = None
    for k in range(d):
        column = upper[k][:, here]
        right = right - exact_dot(column, upper[k][:, low:], ((0,), (0,)))
        term = exact_dot(column, inverse[k][:, :low], ((0,), (0,)))
        left = -term if left is None else left - term
    row_ids = lax.broadcasted_iota(jnp.int32, (BLOCK, BLOCK), 0)
    column_ids = lax.broadcasted_iota(jnp.int32, (BLOCK, BLOCK), 1)
    work[:, :BLOCK] = right[:, :BLOCK]
    work[:, BLOCK:] = (row_ids == column_ids).astype(F32)
    for p in range(0, BLOCK, PIVOTS):
        rows = work[p : p + PIVOTS, :]
        if p:
            rows = rows - exact_dot(work[:p, p : p + PIVOTS], work[:p, :], ((0,), (0,)))
        tiles = [rows[v : v + 8] for v in range(0, PIVOTS, 8)]
        for v, parts in enumerate(eliminate(tiles, p)):
            for q, part in enumerate(parts):
                work[p + 8 * v : p + 8 * v + 8, BLOCK * q : BLOCK * (q + 1)] = part
    block_inverse = work[:, BLOCK:]
    upper_ref[...] = jnp.zeros_like(upper_ref)
    inverse_ref[...] = jnp.zeros_like(inverse_ref)
    upper_ref[:, here] = jnp.where(row_ids <= column_ids, work[:, :BLOCK], 0.0)
    inverse_ref[:, here] = block_inverse
    if low + BLOCK < rank:
        upper_ref[:, low + BLOCK :] = exact_dot(block_inverse, right[:, BLOCK:], ((1,), (0,)))
    if d:
        inverse_ref[:, :low] = exact_dot(block_inverse, left, ((1,), (0,)))


def factor_step(d, gram, upper, inverse):
    rank = gram.shape[1]
    out = jax.ShapeDtypeStruct((BLOCK, rank), F32)
    return pl.pallas_call(
        functools.partial(factor_kernel, d),
        in_specs=[IN_VMEM] * (1 + 2 * d),
        out_specs=(IN_VMEM, IN_VMEM),
        out_shape=(out, out),
        scratch_shapes=[pltpu.VMEM((BLOCK, 2 * BLOCK), F32)],
        compiler_params=params(24),
        cost_estimate=cost(5_000_000_000, 4 * BLOCK * rank * (2 * d + 3)),
        name="factor_step",
    )(gram, *upper, *inverse)


def factorize(gram):
    upper, inverse = [], []
    for d in range(gram.shape[0] // BLOCK):
        up, inv = factor_step(d, gram, upper, inverse)
        upper.append(up)
        inverse.append(inv)
    return jnp.concatenate(upper, 0), inverse


def apply_kernel(scale, core_ref, total_ref, *refs):
    inverse, (kept_ref, away_ref, total, result, sem) = refs[:-5], refs[-5:]
    load = pltpu.make_async_copy(total_ref, total, sem)
    load.start()
    load.wait()
    high, low = split(total[...])
    across = lambda a, b: lax.dot_general(a, b, (((1,), (1,)), ((), ())), preferred_element_type=F32)
    for d, rows_ref in enumerate(inverse):
        end = BLOCK * (d + 1)
        rows_high, rows_low = split(rows_ref[:, :end])
        term = across(rows_high, high[:, :end])
        term += across(rows_high, low[:, :end]) + across(rows_low, high[:, :end])
        result[BLOCK * d : end, :] = term * scale
    count, share, _ = kept_ref.shape
    core = core_ref[0]
    for k in range(count):
        at = lambda part: pl.ds(pl.multiple_of((CS * k + part) * share, share), share)
        kept_ref[k] = result[at(core), :]
        away_ref[k] = result[at(1 - core), :]


def apply_inverse(core, inverse, total, scale):
    cols, rank = total.shape
    out = jax.ShapeDtypeStruct((ZS * XS, rank // (ZS * XS * CS), cols), F32)
    return pl.pallas_call(
        functools.partial(apply_kernel, scale),
        in_specs=[IN_SMEM, IN_PLACE] + [IN_VMEM] * len(inverse),
        out_specs=(IN_VMEM, IN_VMEM),
        out_shape=(out, out),
        scratch_shapes=[
            pltpu.VMEM((cols, rank), F32),
            pltpu.VMEM((rank, cols), F32),
            pltpu.SemaphoreType.DMA,
        ],
        compiler_params=params(24),
        cost_estimate=cost(6 * rank * rank * cols, 8 * rank * (rank + cols)),
        name="apply_inverse",
    )(core, total, *inverse)


def shards(panel, sketch_matrix):
    rank = sketch_matrix.shape[1]
    local_rows, local_cols = panel.shape
    total_rows = local_rows * lax.axis_size("row")
    norm_scale = 1.0 / math.sqrt(total_rows)
    row = lax.axis_index("row")
    c = row % CS
    core, y = c.reshape(1), lax.axis_index("col").reshape(1)
    row_share = rank // (ZS * XS * CS)

    with jax.named_scope("sketch"):
        arrived = swap_core(panel)
        block = local_rows // YS
        half = block // 2
        far = sketch_product(
            y,
            panel,
            sketch_matrix,
            ((2, 0, half), (1, half, half), (3, 0, half), (2, half, half)),
            (block, block),
        )
        far, panel = lax.optimization_barrier((far, panel))
        near = sketch_product(
            y,
            panel,
            sketch_matrix,
            ((1, 0, half), (3, half, half), (0, 0, block)),
            (half, half, block),
        )
        own = place_blocks(y, ring_gather_y(ring_sum_y(*far, *near)))
        other = swap_core(own)

    with jax.named_scope("project"):
        gram, total = chip_products(y, core, own, other, panel, arrived)
        total = lax.psum_scatter(
            total, "row", scatter_dimension=0, axis_index_groups=Z_GROUPS, tiled=True
        )

    with jax.named_scope("gram"):
        gram = exchange(gram, ZX_GROUPS).sum(0)
        gram = exchange(repeat(gram, ZS * XS), ZX_GROUPS).reshape(-1, rank)
        gram = place_blocks(y, ring_gather_y(gram)).reshape(YS, -1, rank)
        gram = place({0: gram, 1: swap_core(gram)}, CS, c)
        gram = gram.transpose(1, 0, 2, 3).reshape(rank, rank)

    with jax.named_scope("factor"):
        upper, inverse = factorize(gram)

    with jax.named_scope("apply"):
        kept, away = apply_inverse(core, inverse, total, norm_scale)
        arrived = swap_core(away)
        first = c == 0
        result = jnp.stack(
            [jnp.where(first, kept, arrived), jnp.where(first, arrived, kept)], axis=1
        )
        result = exchange(result, ZX_GROUPS).reshape(ZS, XS, CS, row_share, -1).sum(1)
        projected = result.transpose(2, 1, 0, 3).reshape(row_share, local_cols)
        spread = lax.dynamic_slice_in_dim(upper, row * row_share, row_share, 0) * norm_scale
    return (projected, spread)


def solution(mesh):
    return jax.shard_map(
        shards,
        mesh=mesh,
        in_specs=(P("row", "col"), P("col", None)),
        out_specs=(P("row", "col"), P("row", None)),
        check_vma=False,
    )
```

```python
import functools
import math

import jax
import jax.numpy as jnp
from jax import lax
from jax.experimental import pallas as pl
from jax.experimental.pallas import tpu as pltpu
from jax.sharding import PartitionSpec as P

ZS, XS, CS, YS = 8, 4, 2, 4
BLOCK = 128
PIVOTS = 16
WIDTH = 512
F32, BF16 = jnp.float32, jnp.bfloat16


def row_index(z, x, c):
    return ((z % ZS) * XS + x % XS) * CS + c


def row_pairs(move):
    return [
        (row_index(z, x, c), row_index(*move(z, x, c)))
        for z in range(ZS)
        for x in range(XS)
        for c in range(CS)
    ]


Z_GROUPS = [[row_index(z, x, c) for z in range(ZS)] for x in range(XS) for c in range(CS)]
ZX_GROUPS = [[row_index(z, x, c) for z in range(ZS) for x in range(XS)] for c in range(CS)]


def send_y(array, step):
    return lax.ppermute(array, "col", [(i, (i + step) % YS) for i in range(YS)])


def swap_core(array):
    return lax.ppermute(array, "row", row_pairs(lambda z, x, c: (z, x, 1 - c)))


def exchange(array, groups):
    return lax.all_to_all(array, "row", 0, 0, axis_index_groups=groups)


def repeat(array, times):
    return jnp.broadcast_to(array[None], (times,) + array.shape)


def together(*arrays):
    return lax.optimization_barrier(arrays)


def ring_sum_y(ahead, behind, next_head, before_tail, own):
    half = own.shape[0] // 2
    from_before, from_after = together(send_y(ahead, 1), send_y(behind, -1))
    head, tail = together(next_head + from_before[:half], before_tail + from_after[half:])
    head, tail = together(send_y(head, 1), send_y(tail, -1))
    return own + jnp.concatenate([from_after[:half] + head, from_before[half:] + tail], 0)


def ring_gather_y(own):
    half = own.shape[0] // 2
    before, after = together(send_y(own, 1), send_y(own, -1))
    return own, before, after, send_y(before[:half], 1), send_y(after[half:], -1)


def place(blocks, size, position):
    own = blocks[0]
    out = jnp.zeros((size,) + own.shape, own.dtype)
    for k, block in blocks.items():
        out = lax.dynamic_update_index_in_dim(out, block, (position + k) % size, 0)
    return out


def split(array):
    high = array.astype(BF16)
    return high, (array - high.astype(F32)).astype(BF16)


def dot(left, right):
    return jnp.dot(left, right, preferred_element_type=F32)


def dot_parts(left, right):
    return dot(left[0], right[0]) + dot(left[0], right[1]) + dot(left[1], right[0])


def params(size):
    return pltpu.CompilerParams(vmem_limit_bytes=size * 2**20)


def cost(flops, size):
    return pl.CostEstimate(flops=flops, bytes_accessed=size, transcendentals=0)


IN_VMEM = pl.BlockSpec(memory_space=pltpu.VMEM)
IN_PLACE = pl.BlockSpec(memory_space=pl.ANY)
IN_SMEM = pl.BlockSpec(memory_space=pltpu.SMEM)


def sketch_kernel(pieces, y_ref, panel_ref, matrix_ref, *refs):
    out_refs, (panels, matrices, total, panel_sems, matrix_sems) = refs[:-5], refs[-5:]
    steps, _, width = panels.shape
    block = panel_ref.shape[0] // YS

    def copies(k):
        at = pl.ds(pl.multiple_of(k * width, width), width)
        out = [pltpu.make_async_copy(matrix_ref.at[at], matrices.at[k], matrix_sems.at[k])]
        offset = 0
        for i, (step, start, size) in enumerate(pieces):
            row = lax.rem(y_ref[0] + step, YS) * block + start
            out.append(
                pltpu.make_async_copy(
                    panel_ref.at[pl.ds(pl.multiple_of(row, block // 2), size), at],
                    panels.at[k, pl.ds(offset, size)],
                    panel_sems.at[k, i],
                )
            )
            offset += size
        return out

    for k in range(steps):
        for copy in copies(k):
            copy.start()
    total[...] = jnp.zeros_like(total)

    def step(k, carry):
        for copy in copies(k):
            copy.wait()
        total[...] += dot_parts(split(panels[k]), split(matrices[k]))
        return carry

    lax.fori_loop(0, steps, step, 0)
    offset = 0
    for out_ref in out_refs:
        size = out_ref.shape[0]
        out_ref[...] = total[offset : offset + size]
        offset += size


def sketch_product(y, panel, matrix, pieces, sizes):
    depth = panel.shape[1]
    rows = sum(sizes)
    rank = matrix.shape[1]
    steps = depth // WIDTH
    return pl.pallas_call(
        functools.partial(sketch_kernel, pieces),
        in_specs=[IN_SMEM, IN_PLACE, IN_PLACE],
        out_specs=(IN_VMEM,) * len(sizes),
        out_shape=tuple(jax.ShapeDtypeStruct((size, rank), F32) for size in sizes),
        scratch_shapes=[
            pltpu.VMEM((steps, rows, WIDTH), F32),
            pltpu.VMEM((steps, WIDTH, rank), F32),
            pltpu.VMEM((rows, rank), F32),
            pltpu.SemaphoreType.DMA((steps, len(pieces))),
            pltpu.SemaphoreType.DMA((steps,)),
        ],
        compiler_params=params(54),
        cost_estimate=cost(6 * rows * rank * depth, 4 * depth * (rows + rank)),
        name="sketch_product",
    )(y, panel, matrix)


def place_kernel(y_ref, own, before, after, head, tail, placed):
    y = y_ref[0]
    at = lambda step: lax.rem(y + step, YS)
    half = placed.shape[1] // 2
    placed[at(0)] = own[...]
    placed[at(3)] = before[...]
    placed[at(1)] = after[...]
    placed[at(2), :half] = head[...]
    placed[at(2), half:] = tail[...]


def place_blocks(y, blocks):
    rows, rank = blocks[0].shape
    return pl.pallas_call(
        place_kernel,
        in_specs=[IN_SMEM] + [IN_VMEM] * 5,
        out_specs=IN_VMEM,
        out_shape=jax.ShapeDtypeStruct((YS, rows, rank), F32),
        compiler_params=params(24),
        cost_estimate=cost(0, 8 * YS * rows * rank),
        name="place_blocks",
    )(y, *blocks).reshape(YS * rows, rank)


def chip_kernel(
    y_ref, core_ref, own_ref, other_ref, panel_ref, arrived_ref, gram_ref, out_ref,
    parts, turned, gram, panels, arrived, outs, panel_sems, arrived_sems, out_sems,
):
    steps, _, width = panels.shape
    base = core_ref[0] * (steps * width)

    def arrive(k):
        at = pl.ds(pl.multiple_of(base + k * width, width), width)
        return (
            pltpu.make_async_copy(panel_ref.at[:, at], panels.at[k], panel_sems.at[k]),
            pltpu.make_async_copy(arrived_ref.at[:, at], arrived.at[k], arrived_sems.at[k]),
        )

    def leave(k):
        at = pl.ds(pl.multiple_of(k * width, width), width)
        return pltpu.make_async_copy(outs.at[k], out_ref.at[at], out_sems.at[k])

    for k in range(steps):
        for copy in arrive(k):
            copy.start()
    share = gram.shape[0]
    block = CS * share
    columns = pl.ds(pl.multiple_of(y_ref[0] * block, block), block)
    for k, sketch_ref in enumerate((own_ref, other_ref)):
        high, low = split(sketch_ref[...])
        parts[2 * k] = high
        parts[2 * k + 1] = low
        turned[...] = sketch_ref[:, columns].T
        rows = turned[pl.ds(pl.multiple_of(core_ref[0] * share, share), share), :]
        term = dot_parts(split(rows), (high, low))
        if k == 0:
            gram[...] = term
        else:
            gram[...] += term
    size = gram_ref.shape[1]
    for k in range(gram_ref.shape[0]):
        gram_ref[k] = gram[size * k : size * (k + 1), :]

    def step(k, carry):
        for copy in arrive(k):
            copy.wait()
        own = dot_parts(split(panels[k].T), (parts[0], parts[1]))
        outs[k] = own + dot_parts(split(arrived[k].T), (parts[2], parts[3]))
        leave(k).start()
        return carry

    lax.fori_loop(0, steps, step, 0)
    for k in range(steps):
        leave(k).wait()


def chip_products(y, core, own, other, panel, arrived):
    rows, rank = own.shape
    share = rank // (YS * CS)
    cols = panel.shape[1] // CS
    steps = cols // WIDTH
    return pl.pallas_call(
        chip_kernel,
        in_specs=[IN_SMEM] * 2 + [IN_VMEM] * 2 + [IN_PLACE] * 2,
        out_specs=(IN_VMEM, IN_PLACE),
        out_shape=(
            jax.ShapeDtypeStruct((ZS * XS, share // (ZS * XS), rank), F32),
            jax.ShapeDtypeStruct((cols, rank), F32),
        ),
        scratch_shapes=[
            pltpu.VMEM((2 * CS, rows, rank), BF16),
            pltpu.VMEM((CS * share, rows), F32),
            pltpu.VMEM((share, rank), F32),
            pltpu.VMEM((steps, rows, WIDTH), F32),
            pltpu.VMEM((steps, rows, WIDTH), F32),
            pltpu.VMEM((steps, WIDTH, rank), F32),
            pltpu.SemaphoreType.DMA((steps,)),
            pltpu.SemaphoreType.DMA((steps,)),
            pltpu.SemaphoreType.DMA((steps,)),
        ],
        compiler_params=params(57),
        cost_estimate=cost(12 * rank * rows * cols, 12 * cols * (rows + rank)),
        name="chip_products",
    )(y, core, own, other, panel, arrived)


def block_dot(left, right, dims):
    left, right = split(left), split(right)
    term = lambda i, j: lax.dot_general(
        left[i], right[j], (dims, ((), ())), preferred_element_type=F32
    )
    return term(0, 0) + term(0, 1) + term(1, 0)


def eliminate(rows, base):
    tiles = len(rows)
    count = 8 * tiles
    lanes = BLOCK
    sub = lax.broadcasted_iota(jnp.int32, (8, lanes), 0)
    spread = lambda a, u: jnp.broadcast_to(a[u : u + 1, :], (8, lanes))
    columns = [
        [jnp.broadcast_to(row[:, base + t : base + t + 1], (8, lanes)) for row in rows]
        for t in range(count)
    ]
    parts = rows[0].shape[1] // lanes
    rows = [[row[:, lanes * q : lanes * (q + 1)] for q in range(parts)] for row in rows]
    scales = []
    for s in range(count):
        first, u = divmod(s, 8)
        if s == 0:
            pivot = spread(columns[0][0], 0)
        scales.append(lax.rsqrt(pivot))
        inverse = 1.0 / pivot
        if s + 1 < count:
            after, at = divmod(s + 1, 8)
            beside = spread(columns[s][after], at)
            pivot = spread(columns[s + 1][after], at) - (beside * inverse) * beside
        factor = {v: columns[s][v] * inverse for v in range(first, tiles)}
        factor[first] = jnp.where(sub > u, factor[first], 0.0)
        for t in range(s + 1, count):
            pivot_row = spread(columns[t][first], u)
            for v in range(first, tiles):
                columns[t][v] = columns[t][v] - factor[v] * pivot_row
        for q in range(parts):
            pivot_row = spread(rows[first][q], u)
            for v in range(first, tiles):
                rows[v][q] = rows[v][q] - factor[v] * pivot_row
    out = []
    for v in range(tiles):
        scale = scales[8 * v]
        for u in range(1, 8):
            scale = jnp.where(sub == u, scales[8 * v + u], scale)
        out.append([part * scale for part in rows[v]])
    return out


def factor_kernel(d, *refs):
    gram_ref, upper, inverse = refs[0], refs[1 : 1 + d], refs[1 + d : 1 + 2 * d]
    upper_ref, inverse_ref, work = refs[1 + 2 * d :]
    rank = gram_ref.shape[1]
    low = BLOCK * d
    here = slice(low, low + BLOCK)
    right = gram_ref[here, low:]
    left = None
    for k in range(d):
        column = upper[k][:, here]
        right = right - block_dot(column, upper[k][:, low:], ((0,), (0,)))
        term = block_dot(column, inverse[k][:, :low], ((0,), (0,)))
        left = -term if left is None else left - term
    row_ids = lax.broadcasted_iota(jnp.int32, (BLOCK, BLOCK), 0)
    column_ids = lax.broadcasted_iota(jnp.int32, (BLOCK, BLOCK), 1)
    work[:, :BLOCK] = right[:, :BLOCK]
    work[:, BLOCK:] = (row_ids == column_ids).astype(F32)
    for p in range(0, BLOCK, PIVOTS):
        rows = work[p : p + PIVOTS, :]
        if p:
            rows = rows - block_dot(work[:p, p : p + PIVOTS], work[:p, :], ((0,), (0,)))
        tiles = [rows[v : v + 8] for v in range(0, PIVOTS, 8)]
        for v, parts in enumerate(eliminate(tiles, p)):
            for q, part in enumerate(parts):
                work[p + 8 * v : p + 8 * v + 8, BLOCK * q : BLOCK * (q + 1)] = part
    block_inverse = work[:, BLOCK:]
    upper_ref[...] = jnp.zeros_like(upper_ref)
    inverse_ref[...] = jnp.zeros_like(inverse_ref)
    upper_ref[:, here] = jnp.where(row_ids <= column_ids, work[:, :BLOCK], 0.0)
    inverse_ref[:, here] = block_inverse
    if low + BLOCK < rank:
        upper_ref[:, low + BLOCK :] = block_dot(block_inverse, right[:, BLOCK:], ((1,), (0,)))
    if d:
        inverse_ref[:, :low] = block_dot(block_inverse, left, ((1,), (0,)))


def factor_step(d, gram, upper, inverse):
    rank = gram.shape[1]
    out = jax.ShapeDtypeStruct((BLOCK, rank), F32)
    return pl.pallas_call(
        functools.partial(factor_kernel, d),
        in_specs=[IN_VMEM] * (1 + 2 * d),
        out_specs=(IN_VMEM, IN_VMEM),
        out_shape=(out, out),
        scratch_shapes=[pltpu.VMEM((BLOCK, 2 * BLOCK), F32)],
        compiler_params=params(24),
        cost_estimate=cost(5_000_000_000, 4 * BLOCK * rank * (2 * d + 3)),
        name="factor_step",
    )(gram, *upper, *inverse)


def factorize(gram):
    upper, inverse = [], []
    for d in range(gram.shape[0] // BLOCK):
        up, inv = factor_step(d, gram, upper, inverse)
        upper.append(up)
        inverse.append(inv)
    return jnp.concatenate(upper, 0), inverse


def apply_kernel(scale, total_ref, *refs):
    inverse, (out_ref, total, sem) = refs[:-3], refs[-3:]
    load = pltpu.make_async_copy(total_ref, total, sem)
    load.start()
    load.wait()
    high, low = split(total[...])
    across = lambda a, b: lax.dot_general(a, b, (((1,), (1,)), ((), ())), preferred_element_type=F32)
    for d, rows_ref in enumerate(inverse):
        end = BLOCK * (d + 1)
        rows_high, rows_low = split(rows_ref[:, :end])
        term = across(rows_high, high[:, :end])
        term += across(rows_high, low[:, :end]) + across(rows_low, high[:, :end])
        out_ref[BLOCK * d : end, :] = term * scale


def apply_inverse(inverse, total, scale):
    cols, rank = total.shape
    return pl.pallas_call(
        functools.partial(apply_kernel, scale),
        in_specs=[IN_PLACE] + [IN_VMEM] * len(inverse),
        out_specs=IN_VMEM,
        out_shape=jax.ShapeDtypeStruct((rank, cols), F32),
        scratch_shapes=[pltpu.VMEM((cols, rank), F32), pltpu.SemaphoreType.DMA],
        compiler_params=params(24),
        cost_estimate=cost(6 * rank * rank * cols, 8 * rank * (rank + cols)),
        name="apply_inverse",
    )(total, *inverse)


def shards(panel, sketch_matrix):
    rank = sketch_matrix.shape[1]
    local_rows, local_cols = panel.shape
    total_rows = local_rows * lax.axis_size("row")
    norm_scale = 1.0 / math.sqrt(total_rows)
    row = lax.axis_index("row")
    c = row % CS
    core, y = c.reshape(1), lax.axis_index("col").reshape(1)
    row_share = rank // (ZS * XS * CS)

    with jax.named_scope("sketch"):
        arrived = swap_core(panel)
        block = local_rows // YS
        half = block // 2
        far = sketch_product(
            y,
            panel,
            sketch_matrix,
            ((2, 0, half), (1, half, half), (3, 0, half), (2, half, half)),
            (block, block),
        )
        far, panel = lax.optimization_barrier((far, panel))
        near = sketch_product(
            y,
            panel,
            sketch_matrix,
            ((1, 0, half), (3, half, half), (0, 0, block)),
            (half, half, block),
        )
        own = place_blocks(y, ring_gather_y(ring_sum_y(*far, *near)))
        other = swap_core(own)

    with jax.named_scope("project"):
        gram, total = chip_products(y, core, own, other, panel, arrived)
        total = lax.psum_scatter(
            total, "row", scatter_dimension=0, axis_index_groups=Z_GROUPS, tiled=True
        )

    with jax.named_scope("gram"):
        gram = exchange(gram, ZX_GROUPS).sum(0)
        gram = exchange(repeat(gram, ZS * XS), ZX_GROUPS).reshape(-1, rank)
        gram = lax.all_to_all(repeat(gram, YS), "col", 0, 0)
        gram = place({0: gram, 1: swap_core(gram)}, CS, c)
        gram = gram.transpose(1, 0, 2, 3).reshape(rank, rank)

    with jax.named_scope("factor"):
        upper, inverse = factorize(gram)

    with jax.named_scope("apply"):
        result = apply_inverse(inverse, total, norm_scale)
        result = exchange(result.reshape(ZS * XS * CS, row_share, -1), None)
        result = result.reshape(ZS, XS, CS, row_share, -1).sum(1)
        projected = result.transpose(2, 1, 0, 3).reshape(row_share, local_cols)
        spread = lax.dynamic_slice_in_dim(upper, row * row_share, row_share, 0) * norm_scale
    return (projected, spread)


def solution(mesh):
    return jax.shard_map(
        shards,
        mesh=mesh,
        in_specs=(P("row", "col"), P("col", None)),
        out_specs=(P("row", "col"), P("row", None)),
        check_vma=False,
    )
```

```python
import functools
import math

import jax
import jax.numpy as jnp
from jax import lax
from jax.experimental import pallas as pl
from jax.experimental.pallas import tpu as pltpu
from jax.sharding import PartitionSpec as P

ZS, XS, CS, YS = 8, 4, 2, 4
BLOCK = 128
PIVOTS = 16
WIDTH = 512
F32, BF16 = jnp.float32, jnp.bfloat16


def row_index(z, x, c):
    return ((z % ZS) * XS + x % XS) * CS + c


def row_pairs(move):
    return [
        (row_index(z, x, c), row_index(*move(z, x, c)))
        for z in range(ZS)
        for x in range(XS)
        for c in range(CS)
    ]


Z_GROUPS = [[row_index(z, x, c) for z in range(ZS)] for x in range(XS) for c in range(CS)]
ZX_GROUPS = [[row_index(z, x, c) for z in range(ZS) for x in range(XS)] for c in range(CS)]


def send_y(array, step):
    return lax.ppermute(array, "col", [(i, (i + step) % YS) for i in range(YS)])


def swap_core(array):
    return lax.ppermute(array, "row", row_pairs(lambda z, x, c: (z, x, 1 - c)))


def exchange(array, groups):
    return lax.all_to_all(array, "row", 0, 0, axis_index_groups=groups)


def repeat(array, times):
    return jnp.broadcast_to(array[None], (times,) + array.shape)


def together(*arrays):
    return lax.optimization_barrier(arrays)


def ring_sum_y(ahead, behind, next_head, before_tail, own):
    half = own.shape[0] // 2
    from_before, from_after = together(send_y(ahead, 1), send_y(behind, -1))
    head, tail = together(next_head + from_before[:half], before_tail + from_after[half:])
    head, tail = together(send_y(head, 1), send_y(tail, -1))
    return own + jnp.concatenate([from_after[:half] + head, from_before[half:] + tail], 0)


def ring_gather_y(own):
    half = own.shape[0] // 2
    before, after = together(send_y(own, 1), send_y(own, -1))
    return own, before, after, send_y(before[:half], 1), send_y(after[half:], -1)


def place(blocks, size, position):
    own = blocks[0]
    out = jnp.zeros((size,) + own.shape, own.dtype)
    for k, block in blocks.items():
        out = lax.dynamic_update_index_in_dim(out, block, (position + k) % size, 0)
    return out


def split(array):
    high = array.astype(BF16)
    return high, (array - high.astype(F32)).astype(BF16)


def dot(left, right):
    return jnp.dot(left, right, preferred_element_type=F32)


def dot_parts(left, right):
    return dot(left[0], right[0]) + dot(left[0], right[1]) + dot(left[1], right[0])


def params(size):
    return pltpu.CompilerParams(vmem_limit_bytes=size * 2**20)


def cost(flops, size):
    return pl.CostEstimate(flops=flops, bytes_accessed=size, transcendentals=0)


IN_VMEM = pl.BlockSpec(memory_space=pltpu.VMEM)
IN_PLACE = pl.BlockSpec(memory_space=pl.ANY)
IN_SMEM = pl.BlockSpec(memory_space=pltpu.SMEM)


def sketch_kernel(pieces, y_ref, panel_ref, matrix_ref, *refs):
    out_refs, (panels, matrices, total, panel_sems, matrix_sems) = refs[:-5], refs[-5:]
    steps, _, width = panels.shape
    block = panel_ref.shape[0] // YS

    def copies(k):
        at = pl.ds(pl.multiple_of(k * width, width), width)
        out = [pltpu.make_async_copy(matrix_ref.at[at], matrices.at[k], matrix_sems.at[k])]
        offset = 0
        for i, (step, start, size) in enumerate(pieces):
            row = lax.rem(y_ref[0] + step, YS) * block + start
            out.append(
                pltpu.make_async_copy(
                    panel_ref.at[pl.ds(pl.multiple_of(row, block // 2), size), at],
                    panels.at[k, pl.ds(offset, size)],
                    panel_sems.at[k, i],
                )
            )
            offset += size
        return out

    for k in range(steps):
        for copy in copies(k):
            copy.start()
    total[...] = jnp.zeros_like(total)

    def step(k, carry):
        for copy in copies(k):
            copy.wait()
        total[...] += dot_parts(split(panels[k]), split(matrices[k]))
        return carry

    lax.fori_loop(0, steps, step, 0)
    offset = 0
    for out_ref in out_refs:
        size = out_ref.shape[0]
        out_ref[...] = total[offset : offset + size]
        offset += size


def sketch_product(y, panel, matrix, pieces, sizes):
    depth = panel.shape[1]
    rows = sum(sizes)
    rank = matrix.shape[1]
    steps = depth // WIDTH
    return pl.pallas_call(
        functools.partial(sketch_kernel, pieces),
        in_specs=[IN_SMEM, IN_PLACE, IN_PLACE],
        out_specs=(IN_VMEM,) * len(sizes),
        out_shape=tuple(jax.ShapeDtypeStruct((size, rank), F32) for size in sizes),
        scratch_shapes=[
            pltpu.VMEM((steps, rows, WIDTH), F32),
            pltpu.VMEM((steps, WIDTH, rank), F32),
            pltpu.VMEM((rows, rank), F32),
            pltpu.SemaphoreType.DMA((steps, len(pieces))),
            pltpu.SemaphoreType.DMA((steps,)),
        ],
        compiler_params=params(54),
        cost_estimate=cost(6 * rows * rank * depth, 4 * depth * (rows + rank)),
        name="sketch_product",
    )(y, panel, matrix)


def place_kernel(y_ref, own, before, after, head, tail, placed):
    y = y_ref[0]
    at = lambda step: lax.rem(y + step, YS)
    half = placed.shape[1] // 2
    placed[at(0)] = own[...]
    placed[at(3)] = before[...]
    placed[at(1)] = after[...]
    placed[at(2), :half] = head[...]
    placed[at(2), half:] = tail[...]


def place_blocks(y, blocks):
    rows, rank = blocks[0].shape
    return pl.pallas_call(
        place_kernel,
        in_specs=[IN_SMEM] + [IN_VMEM] * 5,
        out_specs=IN_VMEM,
        out_shape=jax.ShapeDtypeStruct((YS, rows, rank), F32),
        compiler_params=params(24),
        cost_estimate=cost(0, 8 * YS * rows * rank),
        name="place_blocks",
    )(y, *blocks).reshape(YS * rows, rank)


def chip_kernel(
    y_ref, core_ref, own_ref, other_ref, panel_ref, arrived_ref, gram_ref, out_ref,
    parts, turned, gram, panels, arrived, outs, panel_sems, arrived_sems, out_sems,
):
    steps, _, width = panels.shape
    base = core_ref[0] * (steps * width)

    def arrive(k):
        at = pl.ds(pl.multiple_of(base + k * width, width), width)
        return (
            pltpu.make_async_copy(panel_ref.at[:, at], panels.at[k], panel_sems.at[k]),
            pltpu.make_async_copy(arrived_ref.at[:, at], arrived.at[k], arrived_sems.at[k]),
        )

    def leave(k):
        at = pl.ds(pl.multiple_of(k * width, width), width)
        return pltpu.make_async_copy(outs.at[k], out_ref.at[at], out_sems.at[k])

    for k in range(steps):
        for copy in arrive(k):
            copy.start()
    share = gram.shape[0]
    block = CS * share
    columns = pl.ds(pl.multiple_of(y_ref[0] * block, block), block)
    for k, sketch_ref in enumerate((own_ref, other_ref)):
        high, low = split(sketch_ref[...])
        parts[2 * k] = high
        parts[2 * k + 1] = low
        turned[...] = sketch_ref[:, columns].T
        rows = turned[pl.ds(pl.multiple_of(core_ref[0] * share, share), share), :]
        term = dot_parts(split(rows), (high, low))
        if k == 0:
            gram[...] = term
        else:
            gram[...] += term
    size = gram_ref.shape[1]
    for k in range(gram_ref.shape[0]):
        gram_ref[k] = gram[size * k : size * (k + 1), :]

    def step(k, carry):
        for copy in arrive(k):
            copy.wait()
        own = dot_parts(split(panels[k].T), (parts[0], parts[1]))
        outs[k] = own + dot_parts(split(arrived[k].T), (parts[2], parts[3]))
        leave(k).start()
        return carry

    lax.fori_loop(0, steps, step, 0)
    for k in range(steps):
        leave(k).wait()


def chip_products(y, core, own, other, panel, arrived):
    rows, rank = own.shape
    share = rank // (YS * CS)
    cols = panel.shape[1] // CS
    steps = cols // WIDTH
    return pl.pallas_call(
        chip_kernel,
        in_specs=[IN_SMEM] * 2 + [IN_VMEM] * 2 + [IN_PLACE] * 2,
        out_specs=(IN_VMEM, IN_PLACE),
        out_shape=(
            jax.ShapeDtypeStruct((ZS * XS, share // (ZS * XS), rank), F32),
            jax.ShapeDtypeStruct((cols, rank), F32),
        ),
        scratch_shapes=[
            pltpu.VMEM((2 * CS, rows, rank), BF16),
            pltpu.VMEM((CS * share, rows), F32),
            pltpu.VMEM((share, rank), F32),
            pltpu.VMEM((steps, rows, WIDTH), F32),
            pltpu.VMEM((steps, rows, WIDTH), F32),
            pltpu.VMEM((steps, WIDTH, rank), F32),
            pltpu.SemaphoreType.DMA((steps,)),
            pltpu.SemaphoreType.DMA((steps,)),
            pltpu.SemaphoreType.DMA((steps,)),
        ],
        compiler_params=params(57),
        cost_estimate=cost(12 * rank * rows * cols, 12 * cols * (rows + rank)),
        name="chip_products",
    )(y, core, own, other, panel, arrived)


def block_dot(left, right, dims):
    left, right = split(left), split(right)
    term = lambda i, j: lax.dot_general(
        left[i], right[j], (dims, ((), ())), preferred_element_type=F32
    )
    return term(0, 0) + term(0, 1) + term(1, 0)


def eliminate(rows, base):
    tiles = len(rows)
    count = 8 * tiles
    lanes = BLOCK
    sub = lax.broadcasted_iota(jnp.int32, (8, lanes), 0)
    spread = lambda a, u: jnp.broadcast_to(a[u : u + 1, :], (8, lanes))
    columns = [
        [jnp.broadcast_to(row[:, base + t : base + t + 1], (8, lanes)) for row in rows]
        for t in range(count)
    ]
    parts = rows[0].shape[1] // lanes
    rows = [[row[:, lanes * q : lanes * (q + 1)] for q in range(parts)] for row in rows]
    scales = []
    for s in range(count):
        first, u = divmod(s, 8)
        if s == 0:
            pivot = spread(columns[0][0], 0)
        scales.append(lax.rsqrt(pivot))
        inverse = 1.0 / pivot
        if s + 1 < count:
            after, at = divmod(s + 1, 8)
            beside = spread(columns[s][after], at)
            pivot = spread(columns[s + 1][after], at) - (beside * inverse) * beside
        factor = {v: columns[s][v] * inverse for v in range(first, tiles)}
        factor[first] = jnp.where(sub > u, factor[first], 0.0)
        for t in range(s + 1, count):
            pivot_row = spread(columns[t][first], u)
            for v in range(first, tiles):
                columns[t][v] = columns[t][v] - factor[v] * pivot_row
        for q in range(parts):
            pivot_row = spread(rows[first][q], u)
            for v in range(first, tiles):
                rows[v][q] = rows[v][q] - factor[v] * pivot_row
    out = []
    for v in range(tiles):
        scale = scales[8 * v]
        for u in range(1, 8):
            scale = jnp.where(sub == u, scales[8 * v + u], scale)
        out.append([part * scale for part in rows[v]])
    return out


def apply_block(d, rows_ref, total, scale, out_ref):
    end = BLOCK * (d + 1)
    rows = split(rows_ref[:, :end])
    term = lambda i, j: lax.dot_general(
        rows[i], total[j][:, :end], (((1,), (1,)), ((), ())), preferred_element_type=F32
    )
    out_ref[BLOCK * d : end, :] = (term(0, 0) + term(0, 1) + term(1, 0)) * scale


def factor_kernel(d, scale, *refs):
    gram_ref, upper, inverse = refs[0], refs[1 : 1 + d], refs[1 + d : 1 + 2 * d]
    work, refs = refs[-1], refs[1 + 2 * d : -1]
    if scale is None:
        upper_ref, inverse_ref = refs
    else:
        total_ref, upper_ref, inverse_ref, result_ref = refs
        total = split(total_ref[...])
        for k in range(d):
            apply_block(k, inverse[k], total, scale, result_ref)
    rank = gram_ref.shape[1]
    low = BLOCK * d
    here = slice(low, low + BLOCK)
    right = gram_ref[here, low:]
    left = None
    for k in range(d):
        column = upper[k][:, here]
        right = right - block_dot(column, upper[k][:, low:], ((0,), (0,)))
        term = block_dot(column, inverse[k][:, :low], ((0,), (0,)))
        left = -term if left is None else left - term
    row_ids = lax.broadcasted_iota(jnp.int32, (BLOCK, BLOCK), 0)
    column_ids = lax.broadcasted_iota(jnp.int32, (BLOCK, BLOCK), 1)
    work[:, :BLOCK] = right[:, :BLOCK]
    work[:, BLOCK:] = (row_ids == column_ids).astype(F32)
    for p in range(0, BLOCK, PIVOTS):
        rows = work[p : p + PIVOTS, :]
        if p:
            rows = rows - block_dot(work[:p, p : p + PIVOTS], work[:p, :], ((0,), (0,)))
        tiles = [rows[v : v + 8] for v in range(0, PIVOTS, 8)]
        for v, parts in enumerate(eliminate(tiles, p)):
            for q, part in enumerate(parts):
                work[p + 8 * v : p + 8 * v + 8, BLOCK * q : BLOCK * (q + 1)] = part
    block_inverse = work[:, BLOCK:]
    upper_ref[...] = jnp.zeros_like(upper_ref)
    inverse_ref[...] = jnp.zeros_like(inverse_ref)
    upper_ref[:, here] = jnp.where(row_ids <= column_ids, work[:, :BLOCK], 0.0)
    inverse_ref[:, here] = block_inverse
    if low + BLOCK < rank:
        upper_ref[:, low + BLOCK :] = block_dot(block_inverse, right[:, BLOCK:], ((1,), (0,)))
    if d:
        inverse_ref[:, :low] = block_dot(block_inverse, left, ((1,), (0,)))
    if scale is not None:
        apply_block(d, inverse_ref, total, scale, result_ref)


def factor_step(d, gram, upper, inverse, total=None, scale=None):
    rank = gram.shape[1]
    operands = [gram, *upper, *inverse]
    outs = [jax.ShapeDtypeStruct((BLOCK, rank), F32)] * 2
    if total is not None:
        operands.append(total)
        outs.append(jax.ShapeDtypeStruct((rank, total.shape[0]), F32))
    return pl.pallas_call(
        functools.partial(factor_kernel, d, scale),
        in_specs=[IN_VMEM] * len(operands),
        out_specs=[IN_VMEM] * len(outs),
        out_shape=outs,
        scratch_shapes=[pltpu.VMEM((BLOCK, 2 * BLOCK), F32)],
        compiler_params=params(24),
        cost_estimate=cost(5_000_000_000, 4 * BLOCK * rank * (2 * d + 3)),
        name="factor_step",
    )(*operands)


def factorize(gram, total, scale):
    upper, inverse = [], []
    last = gram.shape[0] // BLOCK - 1
    for d in range(last):
        up, inv = factor_step(d, gram, upper, inverse)
        upper.append(up)
        inverse.append(inv)
    gram, total = together(gram, total)
    up, _, result = factor_step(last, gram, upper, inverse, total, scale)
    return jnp.concatenate([*upper, up], 0), result


def shards(panel, sketch_matrix):
    rank = sketch_matrix.shape[1]
    local_rows, local_cols = panel.shape
    total_rows = local_rows * lax.axis_size("row")
    norm_scale = 1.0 / math.sqrt(total_rows)
    row = lax.axis_index("row")
    c = row % CS
    core, y = c.reshape(1), lax.axis_index("col").reshape(1)
    row_share = rank // (ZS * XS * CS)

    with jax.named_scope("sketch"):
        arrived = swap_core(panel)
        block = local_rows // YS
        half = block // 2
        far = sketch_product(
            y,
            panel,
            sketch_matrix,
            ((2, 0, half), (1, half, half), (3, 0, half), (2, half, half)),
            (block, block),
        )
        far, panel = lax.optimization_barrier((far, panel))
        near = sketch_product(
            y,
            panel,
            sketch_matrix,
            ((1, 0, half), (3, half, half), (0, 0, block)),
            (half, half, block),
        )
        own = place_blocks(y, ring_gather_y(ring_sum_y(*far, *near)))
        other = swap_core(own)

    with jax.named_scope("project"):
        gram, total = chip_products(y, core, own, other, panel, arrived)
        total = lax.psum_scatter(
            total, "row", scatter_dimension=0, axis_index_groups=Z_GROUPS, tiled=True
        )

    with jax.named_scope("gram"):
        gram = exchange(gram, ZX_GROUPS).sum(0)
        gram = exchange(repeat(gram, ZS * XS), ZX_GROUPS).reshape(-1, rank)
        gram = lax.all_to_all(repeat(gram, YS), "col", 0, 0)
        gram = place({0: gram, 1: swap_core(gram)}, CS, c)
        gram = gram.transpose(1, 0, 2, 3).reshape(rank, rank)

    with jax.named_scope("factor"):
        upper, result = factorize(gram, total, norm_scale)

    with jax.named_scope("apply"):
        result = exchange(result.reshape(ZS * XS * CS, row_share, -1), None)
        result = result.reshape(ZS, XS, CS, row_share, -1).sum(1)
        projected = result.transpose(2, 1, 0, 3).reshape(row_share, local_cols)
        spread = lax.dynamic_slice_in_dim(upper, row * row_share, row_share, 0) * norm_scale
    return (projected, spread)


def solution(mesh):
    return jax.shard_map(
        shards,
        mesh=mesh,
        in_specs=(P("row", "col"), P("col", None)),
        out_specs=(P("row", "col"), P("row", None)),
        check_vma=False,
    )
```

```python
import functools
import math

import jax
import jax.numpy as jnp
from jax import lax
from jax.experimental import pallas as pl
from jax.experimental.pallas import tpu as pltpu
from jax.sharding import PartitionSpec as P

ZS, XS, CS, YS = 8, 4, 2, 4
BLOCK = 128
PIVOTS = 16
WIDTH = 512
F32, BF16 = jnp.float32, jnp.bfloat16


def row_index(z, x, c):
    return ((z % ZS) * XS + x % XS) * CS + c


def row_pairs(move):
    return [
        (row_index(z, x, c), row_index(*move(z, x, c)))
        for z in range(ZS)
        for x in range(XS)
        for c in range(CS)
    ]


Z_GROUPS = [[row_index(z, x, c) for z in range(ZS)] for x in range(XS) for c in range(CS)]
ZX_GROUPS = [[row_index(z, x, c) for z in range(ZS) for x in range(XS)] for c in range(CS)]


def send_y(array, step):
    return lax.ppermute(array, "col", [(i, (i + step) % YS) for i in range(YS)])


def swap_core(array):
    return lax.ppermute(array, "row", row_pairs(lambda z, x, c: (z, x, 1 - c)))


def exchange(array, groups):
    return lax.all_to_all(array, "row", 0, 0, axis_index_groups=groups)


def repeat(array, times):
    return jnp.broadcast_to(array[None], (times,) + array.shape)


def together(*arrays):
    return lax.optimization_barrier(arrays)


def ring_sum_y(ahead, behind, next_head, before_tail, own):
    half = own.shape[0] // 2
    from_before, from_after = together(send_y(ahead, 1), send_y(behind, -1))
    head, tail = together(next_head + from_before[:half], before_tail + from_after[half:])
    head, tail = together(send_y(head, 1), send_y(tail, -1))
    return own + jnp.concatenate([from_after[:half] + head, from_before[half:] + tail], 0)


def ring_gather_y(own):
    half = own.shape[0] // 2
    before, after = together(send_y(own, 1), send_y(own, -1))
    return own, before, after, send_y(before[:half], 1), send_y(after[half:], -1)


def place(blocks, size, position):
    own = blocks[0]
    out = jnp.zeros((size,) + own.shape, own.dtype)
    for k, block in blocks.items():
        out = lax.dynamic_update_index_in_dim(out, block, (position + k) % size, 0)
    return out


def split(array):
    high = array.astype(BF16)
    return high, (array - high.astype(F32)).astype(BF16)


def dot(left, right):
    return jnp.dot(left, right, preferred_element_type=F32)


def dot_parts(left, right):
    return dot(left[0], right[0]) + dot(left[0], right[1]) + dot(left[1], right[0])


def params(size):
    return pltpu.CompilerParams(vmem_limit_bytes=size * 2**20)


def cost(flops, size):
    return pl.CostEstimate(flops=flops, bytes_accessed=size, transcendentals=0)


IN_VMEM = pl.BlockSpec(memory_space=pltpu.VMEM)
IN_PLACE = pl.BlockSpec(memory_space=pl.ANY)
IN_SMEM = pl.BlockSpec(memory_space=pltpu.SMEM)


def sketch_kernel(pieces, y_ref, panel_ref, matrix_ref, *refs):
    out_refs, (panels, matrices, total, panel_sems, matrix_sems) = refs[:-5], refs[-5:]
    steps, _, width = panels.shape
    block = panel_ref.shape[0] // YS

    def copies(k):
        at = pl.ds(pl.multiple_of(k * width, width), width)
        out = [pltpu.make_async_copy(matrix_ref.at[at], matrices.at[k], matrix_sems.at[k])]
        offset = 0
        for i, (step, start, size) in enumerate(pieces):
            row = lax.rem(y_ref[0] + step, YS) * block + start
            out.append(
                pltpu.make_async_copy(
                    panel_ref.at[pl.ds(pl.multiple_of(row, block // 2), size), at],
                    panels.at[k, pl.ds(offset, size)],
                    panel_sems.at[k, i],
                )
            )
            offset += size
        return out

    for k in range(steps):
        for copy in copies(k):
            copy.start()
    total[...] = jnp.zeros_like(total)

    def step(k, carry):
        for copy in copies(k):
            copy.wait()
        total[...] += dot_parts(split(panels[k]), split(matrices[k]))
        return carry

    lax.fori_loop(0, steps, step, 0)
    offset = 0
    for out_ref in out_refs:
        size = out_ref.shape[0]
        out_ref[...] = total[offset : offset + size]
        offset += size


def sketch_product(y, panel, matrix, pieces, sizes):
    depth = panel.shape[1]
    rows = sum(sizes)
    rank = matrix.shape[1]
    steps = depth // WIDTH
    return pl.pallas_call(
        functools.partial(sketch_kernel, pieces),
        in_specs=[IN_SMEM, IN_PLACE, IN_PLACE],
        out_specs=(IN_VMEM,) * len(sizes),
        out_shape=tuple(jax.ShapeDtypeStruct((size, rank), F32) for size in sizes),
        scratch_shapes=[
            pltpu.VMEM((steps, rows, WIDTH), F32),
            pltpu.VMEM((steps, WIDTH, rank), F32),
            pltpu.VMEM((rows, rank), F32),
            pltpu.SemaphoreType.DMA((steps, len(pieces))),
            pltpu.SemaphoreType.DMA((steps,)),
        ],
        compiler_params=params(54),
        cost_estimate=cost(6 * rows * rank * depth, 4 * depth * (rows + rank)),
        name="sketch_product",
    )(y, panel, matrix)


def place_kernel(y_ref, own, before, after, head, tail, placed):
    y = y_ref[0]
    at = lambda step: lax.rem(y + step, YS)
    half = placed.shape[1] // 2
    placed[at(0)] = own[...]
    placed[at(3)] = before[...]
    placed[at(1)] = after[...]
    placed[at(2), :half] = head[...]
    placed[at(2), half:] = tail[...]


def place_blocks(y, blocks):
    rows, rank = blocks[0].shape
    return pl.pallas_call(
        place_kernel,
        in_specs=[IN_SMEM] + [IN_VMEM] * 5,
        out_specs=IN_VMEM,
        out_shape=jax.ShapeDtypeStruct((YS, rows, rank), F32),
        compiler_params=params(24),
        cost_estimate=cost(0, 8 * YS * rows * rank),
        name="place_blocks",
    )(y, *blocks).reshape(YS * rows, rank)


def chip_kernel(
    y_ref, core_ref, own_ref, other_ref, panel_ref, arrived_ref, gram_ref, out_ref,
    parts, turned, gram, panels, arrived, outs, panel_sems, arrived_sems, out_sems,
):
    steps, _, width = panels.shape
    base = core_ref[0] * (steps * width)

    def arrive(k):
        at = pl.ds(pl.multiple_of(base + k * width, width), width)
        return (
            pltpu.make_async_copy(panel_ref.at[:, at], panels.at[k], panel_sems.at[k]),
            pltpu.make_async_copy(arrived_ref.at[:, at], arrived.at[k], arrived_sems.at[k]),
        )

    def leave(k):
        at = pl.ds(pl.multiple_of(k * width, width), width)
        return pltpu.make_async_copy(outs.at[k], out_ref.at[at], out_sems.at[k])

    for k in range(steps):
        for copy in arrive(k):
            copy.start()
    share = gram.shape[0]
    block = CS * share
    columns = pl.ds(pl.multiple_of(y_ref[0] * block, block), block)
    for k, sketch_ref in enumerate((own_ref, other_ref)):
        high, low = split(sketch_ref[...])
        parts[2 * k] = high
        parts[2 * k + 1] = low
        turned[...] = sketch_ref[:, columns].T
        rows = turned[pl.ds(pl.multiple_of(core_ref[0] * share, share), share), :]
        term = dot_parts(split(rows), (high, low))
        if k == 0:
            gram[...] = term
        else:
            gram[...] += term
    size = gram_ref.shape[1]
    for k in range(gram_ref.shape[0]):
        gram_ref[k] = gram[size * k : size * (k + 1), :]

    def step(k, carry):
        for copy in arrive(k):
            copy.wait()
        own = dot_parts(split(panels[k].T), (parts[0], parts[1]))
        outs[k] = own + dot_parts(split(arrived[k].T), (parts[2], parts[3]))
        leave(k).start()
        return carry

    lax.fori_loop(0, steps, step, 0)
    for k in range(steps):
        leave(k).wait()


def chip_products(y, core, own, other, panel, arrived):
    rows, rank = own.shape
    share = rank // (YS * CS)
    cols = panel.shape[1] // CS
    steps = cols // WIDTH
    return pl.pallas_call(
        chip_kernel,
        in_specs=[IN_SMEM] * 2 + [IN_VMEM] * 2 + [IN_PLACE] * 2,
        out_specs=(IN_VMEM, IN_PLACE),
        out_shape=(
            jax.ShapeDtypeStruct((ZS * XS, share // (ZS * XS), rank), F32),
            jax.ShapeDtypeStruct((cols, rank), F32),
        ),
        scratch_shapes=[
            pltpu.VMEM((2 * CS, rows, rank), BF16),
            pltpu.VMEM((CS * share, rows), F32),
            pltpu.VMEM((share, rank), F32),
            pltpu.VMEM((steps, rows, WIDTH), F32),
            pltpu.VMEM((steps, rows, WIDTH), F32),
            pltpu.VMEM((steps, WIDTH, rank), F32),
            pltpu.SemaphoreType.DMA((steps,)),
            pltpu.SemaphoreType.DMA((steps,)),
            pltpu.SemaphoreType.DMA((steps,)),
        ],
        compiler_params=params(57),
        cost_estimate=cost(12 * rank * rows * cols, 12 * cols * (rows + rank)),
        name="chip_products",
    )(y, core, own, other, panel, arrived)


def block_dot(left, right, dims):
    left, right = split(left), split(right)
    term = lambda i, j: lax.dot_general(
        left[i], right[j], (dims, ((), ())), preferred_element_type=F32
    )
    return term(0, 0) + term(0, 1) + term(1, 0)


def eliminate(rows, base):
    tiles = len(rows)
    count = 8 * tiles
    lanes = BLOCK
    sub = lax.broadcasted_iota(jnp.int32, (8, lanes), 0)
    spread = lambda a, u: jnp.broadcast_to(a[u : u + 1, :], (8, lanes))
    columns = [
        [jnp.broadcast_to(row[:, base + t : base + t + 1], (8, lanes)) for row in rows]
        for t in range(count)
    ]
    parts = rows[0].shape[1] // lanes
    rows = [[row[:, lanes * q : lanes * (q + 1)] for q in range(parts)] for row in rows]
    scales = []
    for s in range(count):
        first, u = divmod(s, 8)
        if s == 0:
            pivot = spread(columns[0][0], 0)
        scales.append(lax.rsqrt(pivot))
        inverse = 1.0 / pivot
        if s + 1 < count:
            after, at = divmod(s + 1, 8)
            beside = spread(columns[s][after], at)
            pivot = spread(columns[s + 1][after], at) - (beside * inverse) * beside
        factor = {v: columns[s][v] * inverse for v in range(first, tiles)}
        factor[first] = jnp.where(sub > u, factor[first], 0.0)
        for t in range(s + 1, count):
            pivot_row = spread(columns[t][first], u)
            for v in range(first, tiles):
                columns[t][v] = columns[t][v] - factor[v] * pivot_row
        for q in range(parts):
            pivot_row = spread(rows[first][q], u)
            for v in range(first, tiles):
                rows[v][q] = rows[v][q] - factor[v] * pivot_row
    out = []
    for v in range(tiles):
        scale = scales[8 * v]
        for u in range(1, 8):
            scale = jnp.where(sub == u, scales[8 * v + u], scale)
        out.append([part * scale for part in rows[v]])
    return out


def factor_kernel(d, *refs):
    gram_ref, upper, inverse = refs[0], refs[1 : 1 + d], refs[1 + d : 1 + 2 * d]
    upper_ref, inverse_ref, work = refs[1 + 2 * d :]
    rank = gram_ref.shape[1]
    low = BLOCK * d
    here = slice(low, low + BLOCK)
    right = gram_ref[here, low:]
    left = None
    for k in range(d):
        column = upper[k][:, here]
        right = right - block_dot(column, upper[k][:, low:], ((0,), (0,)))
        term = block_dot(column, inverse[k][:, :low], ((0,), (0,)))
        left = -term if left is None else left - term
    row_ids = lax.broadcasted_iota(jnp.int32, (BLOCK, BLOCK), 0)
    column_ids = lax.broadcasted_iota(jnp.int32, (BLOCK, BLOCK), 1)
    work[:, :BLOCK] = right[:, :BLOCK]
    work[:, BLOCK:] = (row_ids == column_ids).astype(F32)
    for p in range(0, BLOCK, PIVOTS):
        rows = work[p : p + PIVOTS, :]
        if p:
            rows = rows - block_dot(work[:p, p : p + PIVOTS], work[:p, :], ((0,), (0,)))
        tiles = [rows[v : v + 8] for v in range(0, PIVOTS, 8)]
        for v, parts in enumerate(eliminate(tiles, p)):
            for q, part in enumerate(parts):
                work[p + 8 * v : p + 8 * v + 8, BLOCK * q : BLOCK * (q + 1)] = part
    block_inverse = work[:, BLOCK:]
    upper_ref[...] = jnp.zeros_like(upper_ref)
    inverse_ref[...] = jnp.zeros_like(inverse_ref)
    upper_ref[:, here] = jnp.where(row_ids <= column_ids, work[:, :BLOCK], 0.0)
    inverse_ref[:, here] = block_inverse
    if low + BLOCK < rank:
        upper_ref[:, low + BLOCK :] = block_dot(block_inverse, right[:, BLOCK:], ((1,), (0,)))
    if d:
        inverse_ref[:, :low] = block_dot(block_inverse, left, ((1,), (0,)))


def factor_step(d, gram, upper, inverse):
    rank = gram.shape[1]
    out = jax.ShapeDtypeStruct((BLOCK, rank), F32)
    return pl.pallas_call(
        functools.partial(factor_kernel, d),
        in_specs=[IN_VMEM] * (1 + 2 * d),
        out_specs=(IN_VMEM, IN_VMEM),
        out_shape=(out, out),
        scratch_shapes=[pltpu.VMEM((BLOCK, 2 * BLOCK), F32)],
        compiler_params=params(24),
        cost_estimate=cost(5_000_000_000, 4 * BLOCK * rank * (2 * d + 3)),
        name="factor_step",
    )(gram, *upper, *inverse)


def factorize(gram, total):
    upper, inverse = [], []
    last = gram.shape[0] // BLOCK - 1
    for d in range(last + 1):
        if d == last:
            gram, total = together(gram, total)
        up, inv = factor_step(d, gram, upper, inverse)
        upper.append(up)
        inverse.append(inv)
    return jnp.concatenate(upper, 0), inverse, total


def apply_kernel(scale, total_ref, *refs):
    inverse, (out_ref, total, sem) = refs[:-3], refs[-3:]
    load = pltpu.make_async_copy(total_ref, total, sem)
    load.start()
    load.wait()
    high, low = split(total[...])
    across = lambda a, b: lax.dot_general(a, b, (((1,), (1,)), ((), ())), preferred_element_type=F32)
    for d, rows_ref in enumerate(inverse):
        end = BLOCK * (d + 1)
        rows_high, rows_low = split(rows_ref[:, :end])
        term = across(rows_high, high[:, :end])
        term += across(rows_high, low[:, :end]) + across(rows_low, high[:, :end])
        out_ref[BLOCK * d : end, :] = term * scale


def apply_inverse(inverse, total, scale):
    cols, rank = total.shape
    return pl.pallas_call(
        functools.partial(apply_kernel, scale),
        in_specs=[IN_PLACE] + [IN_VMEM] * len(inverse),
        out_specs=IN_VMEM,
        out_shape=jax.ShapeDtypeStruct((rank, cols), F32),
        scratch_shapes=[pltpu.VMEM((cols, rank), F32), pltpu.SemaphoreType.DMA],
        compiler_params=params(24),
        cost_estimate=cost(6 * rank * rank * cols, 8 * rank * (rank + cols)),
        name="apply_inverse",
    )(total, *inverse)


def shards(panel, sketch_matrix):
    rank = sketch_matrix.shape[1]
    local_rows, local_cols = panel.shape
    total_rows = local_rows * lax.axis_size("row")
    norm_scale = 1.0 / math.sqrt(total_rows)
    row = lax.axis_index("row")
    c = row % CS
    core, y = c.reshape(1), lax.axis_index("col").reshape(1)
    row_share = rank // (ZS * XS * CS)

    with jax.named_scope("sketch"):
        arrived = swap_core(panel)
        block = local_rows // YS
        half = block // 2
        far = sketch_product(
            y,
            panel,
            sketch_matrix,
            ((2, 0, half), (1, half, half), (3, 0, half), (2, half, half)),
            (block, block),
        )
        far, panel = lax.optimization_barrier((far, panel))
        near = sketch_product(
            y,
            panel,
            sketch_matrix,
            ((1, 0, half), (3, half, half), (0, 0, block)),
            (half, half, block),
        )
        own = place_blocks(y, ring_gather_y(ring_sum_y(*far, *near)))
        other = swap_core(own)

    with jax.named_scope("project"):
        gram, total = chip_products(y, core, own, other, panel, arrived)
        total = lax.psum_scatter(
            total, "row", scatter_dimension=0, axis_index_groups=Z_GROUPS, tiled=True
        )

    with jax.named_scope("gram"):
        gram = exchange(gram, ZX_GROUPS).sum(0)
        gram = exchange(repeat(gram, ZS * XS), ZX_GROUPS).reshape(-1, rank)
        gram = lax.all_to_all(repeat(gram, YS), "col", 0, 0)
        gram = place({0: gram, 1: swap_core(gram)}, CS, c)
        gram = gram.transpose(1, 0, 2, 3).reshape(rank, rank)

    with jax.named_scope("factor"):
        upper, inverse, total = factorize(gram, total)

    with jax.named_scope("apply"):
        result = apply_inverse(inverse, total, norm_scale)
        result = exchange(result.reshape(ZS * XS * CS, row_share, -1), None)
        result = result.reshape(ZS, XS, CS, row_share, -1).sum(1)
        projected = result.transpose(2, 1, 0, 3).reshape(row_share, local_cols)
        spread = lax.dynamic_slice_in_dim(upper, row * row_share, row_share, 0) * norm_scale
    return (projected, spread)


def solution(mesh):
    return jax.shard_map(
        shards,
        mesh=mesh,
        in_specs=(P("row", "col"), P("col", None)),
        out_specs=(P("row", "col"), P("row", None)),
        check_vma=False,
    )
```
